512 devices in a mesh: row: 32 (over y_hi, z), col: 16 (over y_lo, x, core).
Axes of the slice: x: 4, y: 8 (y_hi: 4, y_lo: 2; y = y_hi * 2 + y_lo), z: 8, core: 2. Of those that a mesh axis runs over, the one named last changes fastest.
Arguments:
- density: float32 [16, 1024, 1024], P('col', 'row'), may hold values from 0.3 to 3
- velocity: float32 [3, 16, 1024, 1024], P(None, 'col', 'row'), may hold values from -3 to 3
- pressure: float32 [16, 1024, 1024], P('col', 'row'), may hold values from 0.3 to 3
Outputs:
- conserved: float32 [5, 16, 1024, 1024], P(None, None, ('row', 'col'))
The draws below stay inside these ranges and needn't reach their ends.
All inputs are finite; a program needn't handle non-finite values.
Results may differ from the reference program's by a relative error of at most 0.0003.
Values sent between devices are 32-bit elements; how exact they have to be, the bound alone decides.
No kernel may reach another device: no remote copies, remote signals or barrier semaphores. Data moves between devices by JAX's collectives and lax.ppermute only.
A program may use at most 64 MiB of HBM per device.

```python
import math
import jax
import jax.numpy as jnp
from jax import lax

RITER = 5
NX = 1024
NY = 1024
NZ = 16


def block_scale(rng, dims, shards, low, largest):
    loudness = 1.0
    for dim, parts in shards:
        draws = jax.random.uniform(jax.random.fold_in(jax.random.fold_in(rng, 6), dim), (parts,), jnp.float32, low / len(shards), largest / len(shards))
        loudness = loudness * jnp.repeat(jnp.exp(draws), dims[dim] // parts).reshape((-1,) + (1,) * (len(dims) - 1 - dim))
    return loudness


def noise(key, shape, deviation, limit, split=(), held_as=jnp.bfloat16):
    gain = block_scale(key, shape, split, -0.22, 0.18) if split else 1.0
    array = jax.random.normal(key, shape, jnp.float32) * deviation * gain
    return jnp.minimum(jnp.maximum(array, -limit), limit).astype(held_as)


def setup_inputs(seed: int = 0) -> dict:
    arg_keys = jax.random.split(jax.random.key(seed), 4)
    return {
        "density": jnp.clip(jnp.exp(math.log(3.0) - 2.3025851 * jax.random.uniform(arg_keys[0], (NZ, NY, NX), jnp.float32) ** block_scale(arg_keys[0], (NZ, NY, NX), ((0, 16), (1, 32)), -0.2, 0.2)), 0.3, 3.0),
        "velocity": noise(arg_keys[1], (3, NZ, NY, NX), 0.3, 3.0, ((1, 16), (2, 32)), jnp.float32),
        "pressure": jnp.clip(jnp.exp(math.log(3.0) - 2.3025851 * jax.random.uniform(arg_keys[2], (NZ, NY, NX), jnp.float32) ** block_scale(arg_keys[2], (NZ, NY, NX), ((0, 16), (1, 32)), -0.2, 0.2)), 0.3, 3.0),
    }


ADIABATIC = 5.0 / 3.0
COURANT_NUMBER = 0.3
PRESSURE_FLOOR = 0.05

def to_fields(density, velocity, pressure):
    moment = density[None] * velocity
    energy = pressure / (ADIABATIC - 1.0) + 0.5 * density * lax.optimization_barrier(jnp.sum(velocity * velocity, axis=0))
    return jnp.concatenate([density[None], moment, energy[None]], axis=0)

def signal_speed(density, velocity, pressure):
    sound = jnp.sqrt(ADIABATIC * pressure / density)
    return jnp.max(lax.optimization_barrier(jnp.max(jnp.abs(velocity), axis=0)) + sound)

def sweep_line(fields, line_axis, normal, step_size):
    cell_axis = line_axis - 1
    mass_now = fields[0]
    moment = fields[1:4]
    energy = fields[4]
    speeds = moment / mass_now[None]
    press_now = jnp.maximum((ADIABATIC - 1.0) * (energy - 0.5 * mass_now * lax.optimization_barrier(jnp.sum(speeds * speeds, axis=0))), PRESSURE_FLOOR)
    along = speeds[normal - 1]
    sound = jnp.sqrt(ADIABATIC * press_now / mass_now)
    reach = sound * step_size

    def traced(values):
        upper = jnp.roll(values, -1, cell_axis)
        face_value = 7.0 / 12.0 * (values + upper) - 1.0 / 12.0 * (jnp.roll(values, 1, cell_axis) + jnp.roll(values, -2, cell_axis))
        face_value = jnp.clip(face_value, jnp.minimum(values, upper), jnp.maximum(values, upper))
        left_edge = jnp.roll(face_value, 1, cell_axis)
        slope = face_value - left_edge
        curve = 6.0 * (values - 0.5 * (left_edge + face_value))
        weight = 1.0 - 2.0 / 3.0 * reach
        from_left = face_value - 0.5 * reach * (slope - weight * curve)
        from_right = jnp.roll(left_edge + 0.5 * reach * (slope + weight * curve), -1, cell_axis)
        return (from_left, from_right)
    mass_left, mass_right = traced(mass_now)
    mass_left = jnp.maximum(mass_left, PRESSURE_FLOOR)
    mass_right = jnp.maximum(mass_right, PRESSURE_FLOOR)
    speed_left, speed_right = traced(along)
    press_left, press_right = traced(press_now)
    press_left = jnp.maximum(press_left, PRESSURE_FLOOR)
    press_right = jnp.maximum(press_right, PRESSURE_FLOOR)
    imped_left = jnp.sqrt(ADIABATIC * press_left * mass_left)
    imped_right = jnp.sqrt(ADIABATIC * press_right * mass_right)
    star_press = (imped_right * press_left + imped_left * press_right + imped_left * imped_right * (speed_left - speed_right)) / (imped_left + imped_right)
    star_press = jnp.maximum(star_press, PRESSURE_FLOOR)
    factor = (ADIABATIC + 1.0) / (2.0 * ADIABATIC)

    def waves(star_press):
        wave_left = imped_left * jnp.sqrt(1.0 + factor * (star_press / press_left - 1.0))
        wave_right = imped_right * jnp.sqrt(1.0 + factor * (star_press / press_right - 1.0))
        star_left = speed_left - (star_press - press_left) / wave_left
        star_right = speed_right + (star_press - press_right) / wave_right
        return (wave_left, wave_right, star_left, star_right)
    for turn in range(RITER):
        wave_left, wave_right, star_left, star_right = waves(star_press)
        slope_left = 2.0 * wave_left ** 3 / (wave_left * wave_left + imped_left * imped_left)
        slope_right = 2.0 * wave_right ** 3 / (wave_right * wave_right + imped_right * imped_right)
        star_press = jnp.maximum(star_press - slope_left * slope_right * (star_right - star_left) / (slope_left + slope_right), PRESSURE_FLOOR)
    wave_left, wave_right, star_left, star_right = waves(star_press)
    star_speed = (wave_left * star_left + wave_right * star_right) / (wave_left + wave_right)
    volume = 1.0 + step_size * (star_speed - jnp.roll(star_speed, 1, cell_axis))
    new_along = along - step_size * (star_press - jnp.roll(star_press, 1, cell_axis)) / mass_now
    work_flux = star_press * star_speed
    specific = energy / mass_now - step_size * (work_flux - jnp.roll(work_flux, 1, cell_axis)) / mass_now
    amounts = [mass_now, moment[0], moment[1], moment[2], mass_now * specific]
    amounts[normal] = mass_now * new_along
    amounts = jnp.stack(amounts, axis=0)
    shift = step_size * star_speed
    per_volume = amounts / volume[None]
    donor = jnp.where(shift[None] > 0.0, per_volume, jnp.roll(per_volume, -1, line_axis))
    flux = shift[None] * donor
    return amounts - flux + jnp.roll(flux, 1, line_axis)

def reference(density, velocity, pressure):
    step_size = COURANT_NUMBER / signal_speed(density, velocity, pressure)
    fields = to_fields(density, velocity, pressure)
    planes = jnp.moveaxis(fields, 1, 0)
    planes = lax.map(lambda plane: sweep_line(sweep_line(plane, 2, 1, step_size), 1, 2, step_size), planes)
    fields = jnp.moveaxis(planes, 0, 1)
    columns = jnp.moveaxis(fields, 2, 0)
    columns = lax.map(lambda column: sweep_line(column, 1, 3, step_size), columns)
    return jnp.moveaxis(columns, 0, 2)
```

```python
import jax
import jax.numpy as jnp
from jax import lax
from jax.experimental import pallas as pl
from jax.experimental.pallas import tpu as pltpu
from jax.sharding import PartitionSpec as P

RITER = 5
ADIABATIC = 5.0 / 3.0
COURANT_NUMBER = 0.3
PRESSURE_FLOOR = 0.05

LINES = 8
LANES = 128
HALO = 4
F32 = jnp.float32


def inverse(value):
    return pl.reciprocal(value, approx=False)


def faces(before, here, after, beyond):
    value = 7.0 / 12.0 * (here + after) - 1.0 / 12.0 * (before + beyond)
    return jnp.minimum(jnp.maximum(value, jnp.minimum(here, after)), jnp.maximum(here, after))


def traced(here, lower, upper, half_reach):
    slope = upper - lower
    curve = 6.0 * here - 3.0 * (lower + upper)
    bend = (1.0 - 4.0 / 3.0 * half_reach) * curve
    return upper - half_reach * (slope - bend), lower + half_reach * (slope + bend)


def riemann(mass_l, speed_l, press_l, mass_r, speed_r, press_r):
    square_l = ADIABATIC * press_l * mass_l
    square_r = ADIABATIC * press_r * mass_r
    gain_l = 0.5 * (ADIABATIC + 1.0) * mass_l
    gain_r = 0.5 * (ADIABATIC + 1.0) * mass_r
    imped_l = square_l * lax.rsqrt(square_l)
    imped_r = square_r * lax.rsqrt(square_r)
    closing = speed_l - speed_r
    star = (imped_r * press_l + imped_l * press_r + imped_l * imped_r * closing) * inverse(imped_l + imped_r)
    star = jnp.maximum(star, PRESSURE_FLOOR)
    for _ in range(RITER):
        jump_l = star - press_l
        jump_r = star - press_r
        root_l = lax.rsqrt(gain_l * jump_l + square_l)
        root_r = lax.rsqrt(gain_r * jump_r + square_r)
        gap = closing - jump_l * root_l - jump_r * root_r
        bottom = root_l * (1.0 + square_l * (root_l * root_l)) + root_r * (1.0 + square_r * (root_r * root_r))
        star = jnp.maximum(star + 2.0 * gap * inverse(bottom), PRESSURE_FLOOR)
    wave_l = gain_l * (star - press_l) + square_l
    wave_r = gain_r * (star - press_r) + square_r
    wave_l = wave_l * lax.rsqrt(wave_l)
    wave_r = wave_r * lax.rsqrt(wave_r)
    speed = (wave_l * speed_l + wave_r * speed_r + (press_l - press_r)) * inverse(wave_l + wave_r)
    return star, speed


def primitives(mass, moments, energy, normal, step):
    thin = inverse(mass)
    square = moments[0] * moments[0] + moments[1] * moments[1] + moments[2] * moments[2]
    press = jnp.maximum((ADIABATIC - 1.0) * (energy - 0.5 * square * thin), PRESSURE_FLOOR)
    sound = ADIABATIC * press * thin
    return moments[normal] * thin, press, 0.5 * step * (sound * lax.rsqrt(sound))


def interfaces(mass, speed, press, half_reach):
    sides = []
    n = mass.shape[0] - 5
    for value in (mass, speed, press):
        face = faces(value[: n + 2], value[1 : n + 3], value[2 : n + 4], value[3 : n + 5])
        up, down = traced(value[2 : n + 3], face[: n + 1], face[1:], half_reach[2 : n + 3])
        sides.append((up[:n], down[1:]))
    (mass_l, mass_r), (speed_l, speed_r), (press_l, press_r) = sides
    return riemann(
        jnp.maximum(mass_l, PRESSURE_FLOOR),
        speed_l,
        jnp.maximum(press_l, PRESSURE_FLOOR),
        jnp.maximum(mass_r, PRESSURE_FLOOR),
        speed_r,
        jnp.maximum(press_r, PRESSURE_FLOOR),
    )


def remap(fields, normal, star, speed, step):
    n = star.shape[0] - 3
    shift = step * speed
    work = shift * star
    thin = inverse(1.0 + (shift[1:] - shift[:-1]))
    push = step * (star[1:] - star[:-1])
    amounts = list(fields)
    amounts[normal] = fields[normal] - push
    amounts[4] = fields[4] - (work[1:] - work[:-1])
    ahead = jnp.maximum(shift[1:-1], 0.0) * thin[:-1]
    back = jnp.minimum(shift[1:-1], 0.0) * thin[1:]
    keep = 1.0 - ahead[1:] + back[:-1]
    return [a[1 : n + 1] * keep + a[:n] * ahead[:-1] - a[2:] * back[1:] for a in amounts]


def shift_up(value):
    lane = lax.broadcasted_iota(jnp.int32, value.shape, value.ndim - 1)
    next_line = pltpu.roll(value, LINES - 1, value.ndim - 2)
    return pltpu.roll(jnp.where(lane == 0, next_line, value), LANES - 1, value.ndim - 1)


def shift_down(value):
    lane = lax.broadcasted_iota(jnp.int32, value.shape, value.ndim - 1)
    last_line = pltpu.roll(value, 1, value.ndim - 2)
    return pltpu.roll(jnp.where(lane == LANES - 1, last_line, value), 1, value.ndim - 1)


def sweep_x(mass, speeds, press, step):
    press = jnp.maximum(press, PRESSURE_FLOOR)
    moments = [mass * v for v in speeds]
    square = speeds[0] * speeds[0] + speeds[1] * speeds[1] + speeds[2] * speeds[2]
    energy = 1.0 / (ADIABATIC - 1.0) * press + 0.5 * mass * square
    sound = ADIABATIC * press * inverse(mass)
    half_reach = 0.5 * step * (sound * lax.rsqrt(sound))
    sides = []
    for value in (mass, speeds[0], press):
        after = shift_up(value)
        face = faces(shift_down(value), value, after, shift_up(after))
        up, down = traced(value, shift_down(face), face, half_reach)
        sides.append((up, shift_up(down)))
    (mass_l, mass_r), (speed_l, speed_r), (press_l, press_r) = sides
    star, speed = riemann(
        jnp.maximum(mass_l, PRESSURE_FLOOR),
        speed_l,
        jnp.maximum(press_l, PRESSURE_FLOOR),
        jnp.maximum(mass_r, PRESSURE_FLOOR),
        speed_r,
        jnp.maximum(press_r, PRESSURE_FLOOR),
    )
    shift = step * speed
    work = shift * star
    thin = inverse(1.0 + (shift - shift_down(shift)))
    push = step * (star - shift_down(star))
    amounts = [mass, moments[0] - push, moments[1], moments[2], energy - (work - shift_down(work))]
    ahead = jnp.maximum(shift, 0.0) * thin
    back = jnp.minimum(shift, 0.0) * shift_up(thin)
    flux = [ahead * a + back * shift_up(a) for a in amounts]
    return [a - f + shift_down(f) for a, f in zip(amounts, flux)]


def row_of(ref, row):
    return ref[pl.ds((row // LINES) * LINES * LINES + row % LINES, LINES, stride=LINES), :]


def survey_kernel(density, velocity, pressure, speed, low, high):
    mass, press = density[...], pressure[...]
    sound = ADIABATIC * press / mass
    largest = jnp.maximum(jnp.abs(velocity[0]), jnp.abs(velocity[1]))
    largest = jnp.maximum(largest, jnp.abs(velocity[2])) + sound * lax.rsqrt(sound)
    speed[0, 0] = jnp.max(largest)
    refs = (density, velocity.at[0], velocity.at[1], velocity.at[2], pressure)
    for index, ref in enumerate(refs):
        for row in range(HALO):
            low[index, row] = row_of(ref, row)
            high[index, row] = row_of(ref, 32 - HALO + row)


X_ROWS = 8
Y_FACES = 7
Y_CELLS = 8


def plane_kernel(top, density, velocity, pressure, below, above, out, raw, fields, prims, star, speed):
    step = COURANT_NUMBER / jnp.full((LINES, LANES), top[0, 0], F32)
    refs = (density, velocity.at[0], velocity.at[1], velocity.at[2], pressure)
    for index, ref in enumerate(refs):
        raw[index, 0:HALO] = below[index]
        raw[index, 32 + HALO : 32 + 2 * HALO] = above[index]
        for row in range(32):
            raw[index, HALO + row] = row_of(ref, row)

    @pl.loop(0, 40 // X_ROWS)
    def _(block):
        rows = pl.ds(block * X_ROWS, X_ROWS)
        got = [raw[index, rows] for index in range(5)]
        new = sweep_x(got[0], got[1:4], got[4], step)
        for index in range(5):
            fields[index, rows] = new[index]
        along, press, half_reach = primitives(new[0], new[1:4], new[4], 1, step)
        prims[0, rows] = along
        prims[1, rows] = press
        prims[2, rows] = half_reach

    @pl.loop(0, 35 // Y_FACES)
    def _(block):
        rows = pl.ds(block * Y_FACES, Y_FACES + 5)
        s, u = interfaces(fields[0, rows], prims[0, rows], prims[1, rows], prims[2, rows])
        star[pl.ds(block * Y_FACES, Y_FACES)] = s
        speed[pl.ds(block * Y_FACES, Y_FACES)] = u

    @pl.loop(0, 32 // Y_CELLS)
    def _(block):
        first = block * Y_CELLS
        rows = pl.ds(first + HALO - 1, Y_CELLS + 2)
        near = pl.ds(first, Y_CELLS + 3)
        new = remap([fields[index, rows] for index in range(5)], 2, star[near], speed[near], step)
        for index in range(5):
            out[pl.ds(block * (Y_CELLS // 2), Y_CELLS // 2), 2 * index : 2 * index + 2] = new[index].reshape(
                Y_CELLS // 2, 2, LINES, LANES
            )


Z_FACES = 8


def column_kernel(top, lines, out, prims, star, speed):
    step = COURANT_NUMBER / jnp.full((LINES, LANES), top[0, 0], F32)

    @pl.loop(0, 2)
    def _(row):
        fields = [lines[:, 2 * index + row] for index in range(5)]
        along, press, half_reach = primitives(fields[0], fields[1:4], fields[4], 2, step)
        for index, value in enumerate((fields[0], along, press, half_reach)):
            prims[index, 2:18] = value
            prims[index, 0:2] = value[14:16]
            prims[index, 18:21] = value[0:3]

        @pl.loop(0, 16 // Z_FACES)
        def _(block):
            cells = pl.ds(block * Z_FACES, Z_FACES + 5)
            s, u = interfaces(*(prims[index, cells] for index in range(4)))
            star[pl.ds(block * Z_FACES, Z_FACES)] = s
            speed[pl.ds(block * Z_FACES, Z_FACES)] = u

        def ring(value, before, after):
            return jnp.concatenate([value[16 - before :], value, value[:after]], axis=0)

        new = remap(
            [ring(f, 1, 1) for f in fields], 3, ring(star[...], 2, 1), ring(speed[...], 2, 1), step
        )
        for index in range(5):
            for z in range(16):
                out[index, z, pl.ds(row, LINES, stride=2), :] = new[index][z]


def tiled(array):
    lead = array.shape[:-2]
    split = array.reshape(lead + (4, LINES, LINES, LANES))
    return jnp.swapaxes(split, -3, -2).reshape(lead + (256, LANES))


def local(density, velocity, pressure, rows, cols):
    vmem = pl.BlockSpec(memory_space=pltpu.VMEM)
    smem = pl.BlockSpec(memory_space=pltpu.SMEM)
    density = tiled(density[0])
    velocity = tiled(velocity[:, 0])
    pressure = tiled(pressure[0])
    halo = jax.ShapeDtypeStruct((5, HALO, LINES, LANES), F32)
    fastest, low, high = pl.pallas_call(
        survey_kernel,
        out_shape=(jax.ShapeDtypeStruct((1, 1), F32), halo, halo),
        in_specs=[vmem] * 3,
        out_specs=(smem, vmem, vmem),
        name="survey",
    )(density, velocity, pressure)
    below = lax.ppermute(high, "row", [(i, (i + 1) % rows) for i in range(rows)])
    above = lax.ppermute(low, "row", [(i, (i - 1) % rows) for i in range(rows)])
    top = lax.pmax(fastest[0, 0], ("row", "col")).reshape(1, 1)
    lines = pl.pallas_call(
        plane_kernel,
        out_shape=jax.ShapeDtypeStruct((16, 10, LINES, LANES), F32),
        in_specs=[smem] + [vmem] * 5,
        out_specs=vmem,
        scratch_shapes=[
            pltpu.VMEM((5, 40, LINES, LANES), F32),
            pltpu.VMEM((5, 40, LINES, LANES), F32),
            pltpu.VMEM((3, 40, LINES, LANES), F32),
            pltpu.VMEM((35, LINES, LANES), F32),
            pltpu.VMEM((35, LINES, LANES), F32),
        ],
        compiler_params=pltpu.CompilerParams(vmem_limit_bytes=32 * 1024 * 1024),
        name="plane_sweeps",
    )(top, density, velocity, pressure, below, above)
    lines = lax.all_to_all(lines, "col", split_axis=0, concat_axis=0, tiled=True)
    result = pl.pallas_call(
        column_kernel,
        out_shape=jax.ShapeDtypeStruct((5, 16, 16, LANES), F32),
        in_specs=[smem, vmem],
        out_specs=vmem,
        scratch_shapes=[
            pltpu.VMEM((4, 21, LINES, LANES), F32),
            pltpu.VMEM((16, LINES, LANES), F32),
            pltpu.VMEM((16, LINES, LANES), F32),
        ],
        compiler_params=pltpu.CompilerParams(vmem_limit_bytes=32 * 1024 * 1024),
        name="column_sweep",
    )(top, lines)
    return jnp.swapaxes(result.reshape(5, 16, LINES, 2, LANES), 2, 3).reshape(5, 16, 2, LINES * LANES)


def solution(mesh):
    rows, cols = mesh.shape["row"], mesh.shape["col"]
    placed = (P("col", "row", None), P(None, "col", "row", None), P("col", "row", None))

    def step(density, velocity, pressure):
        return local(density, velocity, pressure, rows, cols)

    return jax.shard_map(
        step,
        mesh=mesh,
        in_specs=placed,
        out_specs=P(None, None, ("row", "col"), None),
        check_vma=False,
    )
```

```python
import jax
import jax.numpy as jnp
from jax import lax
from jax.experimental import pallas as pl
from jax.experimental.pallas import tpu as pltpu
from jax.sharding import PartitionSpec as P

RITER = 5
ADIABATIC = 5.0 / 3.0
COURANT_NUMBER = 0.3
PRESSURE_FLOOR = 0.05

LINES = 8
LANES = 128
HALO = 4
F32 = jnp.float32


def inverse(value):
    return pl.reciprocal(value, approx=False)


def faces(before, here, after, beyond):
    value = 7.0 / 12.0 * (here + after) - 1.0 / 12.0 * (before + beyond)
    return jnp.minimum(jnp.maximum(value, jnp.minimum(here, after)), jnp.maximum(here, after))


def traced(here, lower, upper, half_reach):
    slope = upper - lower
    curve = 6.0 * here - 3.0 * (lower + upper)
    bend = (1.0 - 4.0 / 3.0 * half_reach) * curve
    return upper - half_reach * (slope - bend), lower + half_reach * (slope + bend)


def riemann(mass_l, speed_l, press_l, mass_r, speed_r, press_r):
    square_l = ADIABATIC * press_l * mass_l
    square_r = ADIABATIC * press_r * mass_r
    gain_l = 0.5 * (ADIABATIC + 1.0) * mass_l
    gain_r = 0.5 * (ADIABATIC + 1.0) * mass_r
    imped_l = square_l * lax.rsqrt(square_l)
    imped_r = square_r * lax.rsqrt(square_r)
    closing = speed_l - speed_r
    star = (imped_r * press_l + imped_l * press_r + imped_l * imped_r * closing) * inverse(imped_l + imped_r)
    star = jnp.maximum(star, PRESSURE_FLOOR)
    for _ in range(RITER):
        jump_l = star - press_l
        jump_r = star - press_r
        root_l = lax.rsqrt(gain_l * jump_l + square_l)
        root_r = lax.rsqrt(gain_r * jump_r + square_r)
        gap = closing - jump_l * root_l - jump_r * root_r
        bottom = root_l * (1.0 + square_l * (root_l * root_l)) + root_r * (1.0 + square_r * (root_r * root_r))
        star = jnp.maximum(star + 2.0 * gap * inverse(bottom), PRESSURE_FLOOR)
    wave_l = gain_l * (star - press_l) + square_l
    wave_r = gain_r * (star - press_r) + square_r
    wave_l = wave_l * lax.rsqrt(wave_l)
    wave_r = wave_r * lax.rsqrt(wave_r)
    speed = (wave_l * speed_l + wave_r * speed_r + (press_l - press_r)) * inverse(wave_l + wave_r)
    return star, speed


def primitives(mass, moments, energy, normal, step):
    thin = inverse(mass)
    square = moments[0] * moments[0] + moments[1] * moments[1] + moments[2] * moments[2]
    press = jnp.maximum((ADIABATIC - 1.0) * (energy - 0.5 * square * thin), PRESSURE_FLOOR)
    sound = ADIABATIC * press * thin
    return moments[normal] * thin, press, 0.5 * step * (sound * lax.rsqrt(sound))


def interfaces(mass, speed, press, half_reach):
    sides = []
    n = mass.shape[0] - 5
    for value in (mass, speed, press):
        face = faces(value[: n + 2], value[1 : n + 3], value[2 : n + 4], value[3 : n + 5])
        up, down = traced(value[2 : n + 3], face[: n + 1], face[1:], half_reach[2 : n + 3])
        sides.append((up[:n], down[1:]))
    (mass_l, mass_r), (speed_l, speed_r), (press_l, press_r) = sides
    return riemann(
        jnp.maximum(mass_l, PRESSURE_FLOOR),
        speed_l,
        jnp.maximum(press_l, PRESSURE_FLOOR),
        jnp.maximum(mass_r, PRESSURE_FLOOR),
        speed_r,
        jnp.maximum(press_r, PRESSURE_FLOOR),
    )


def remap(fields, normal, star, speed, step):
    n = star.shape[0] - 3
    shift = step * speed
    work = shift * star
    thin = inverse(1.0 + (shift[1:] - shift[:-1]))
    push = step * (star[1:] - star[:-1])
    amounts = list(fields)
    amounts[normal] = fields[normal] - push
    amounts[4] = fields[4] - (work[1:] - work[:-1])
    ahead = jnp.maximum(shift[1:-1], 0.0) * thin[:-1]
    back = jnp.minimum(shift[1:-1], 0.0) * thin[1:]
    keep = 1.0 - ahead[1:] + back[:-1]
    return [a[1 : n + 1] * keep + a[:n] * ahead[:-1] - a[2:] * back[1:] for a in amounts]


def shift_up(value):
    lane = lax.broadcasted_iota(jnp.int32, value.shape, value.ndim - 1)
    next_line = pltpu.roll(value, LINES - 1, value.ndim - 2)
    return pltpu.roll(jnp.where(lane == 0, next_line, value), LANES - 1, value.ndim - 1)


def shift_down(value):
    lane = lax.broadcasted_iota(jnp.int32, value.shape, value.ndim - 1)
    last_line = pltpu.roll(value, 1, value.ndim - 2)
    return pltpu.roll(jnp.where(lane == LANES - 1, last_line, value), 1, value.ndim - 1)


def sweep_x(mass, speeds, press, step):
    press = jnp.maximum(press, PRESSURE_FLOOR)
    moments = [mass * v for v in speeds]
    square = speeds[0] * speeds[0] + speeds[1] * speeds[1] + speeds[2] * speeds[2]
    energy = 1.0 / (ADIABATIC - 1.0) * press + 0.5 * mass * square
    sound = ADIABATIC * press * inverse(mass)
    half_reach = 0.5 * step * (sound * lax.rsqrt(sound))
    sides = []
    for value in (mass, speeds[0], press):
        after = shift_up(value)
        face = faces(shift_down(value), value, after, shift_up(after))
        up, down = traced(value, shift_down(face), face, half_reach)
        sides.append((up, shift_up(down)))
    (mass_l, mass_r), (speed_l, speed_r), (press_l, press_r) = sides
    star, speed = riemann(
        jnp.maximum(mass_l, PRESSURE_FLOOR),
        speed_l,
        jnp.maximum(press_l, PRESSURE_FLOOR),
        jnp.maximum(mass_r, PRESSURE_FLOOR),
        speed_r,
        jnp.maximum(press_r, PRESSURE_FLOOR),
    )
    shift = step * speed
    work = shift * star
    thin = inverse(1.0 + (shift - shift_down(shift)))
    push = step * (star - shift_down(star))
    amounts = [mass, moments[0] - push, moments[1], moments[2], energy - (work - shift_down(work))]
    ahead = jnp.maximum(shift, 0.0) * thin
    back = jnp.minimum(shift, 0.0) * shift_up(thin)
    flux = [ahead * a + back * shift_up(a) for a in amounts]
    return [a - f + shift_down(f) for a, f in zip(amounts, flux)]


def row_of(ref, row):
    return ref[pl.ds((row // LINES) * LINES * LINES + row % LINES, LINES, stride=LINES), :]


def survey_kernel(density, velocity, pressure, speed, low, high):
    mass, press = density[...], pressure[...]
    sound = ADIABATIC * press / mass
    largest = jnp.maximum(jnp.abs(velocity[0]), jnp.abs(velocity[1]))
    largest = jnp.maximum(largest, jnp.abs(velocity[2])) + sound * lax.rsqrt(sound)
    speed[...] = jnp.full(speed.shape, jnp.max(largest), F32)
    refs = (density, velocity.at[0], velocity.at[1], velocity.at[2], pressure)
    for index, ref in enumerate(refs):
        for row in range(HALO):
            low[index, row] = row_of(ref, row)
            high[index, row] = row_of(ref, 32 - HALO + row)


def gather_kernel(speeds, speed):
    speed[...] = jnp.broadcast_to(jnp.max(speeds[...], axis=0, keepdims=True), speed.shape)


def step_of(speeds):
    return COURANT_NUMBER / jnp.broadcast_to(jnp.max(speeds[...], axis=0, keepdims=True), (LINES, LANES))


X_ROWS = 8
Y_FACES = 7
Y_CELLS = 8


def plane_kernel(top, density, velocity, pressure, below, above, out, raw, fields, prims, star, speed):
    step = step_of(top)
    refs = (density, velocity.at[0], velocity.at[1], velocity.at[2], pressure)
    for index, ref in enumerate(refs):
        raw[index, 0:HALO] = below[index]
        raw[index, 32 + HALO : 32 + 2 * HALO] = above[index]
        for row in range(32):
            raw[index, HALO + row] = row_of(ref, row)

    @pl.loop(0, 40 // X_ROWS)
    def _(block):
        rows = pl.ds(block * X_ROWS, X_ROWS)
        got = [raw[index, rows] for index in range(5)]
        new = sweep_x(got[0], got[1:4], got[4], step)
        for index in range(5):
            fields[index, rows] = new[index]
        along, press, half_reach = primitives(new[0], new[1:4], new[4], 1, step)
        prims[0, rows] = along
        prims[1, rows] = press
        prims[2, rows] = half_reach

    @pl.loop(0, 35 // Y_FACES)
    def _(block):
        rows = pl.ds(block * Y_FACES, Y_FACES + 5)
        s, u = interfaces(fields[0, rows], prims[0, rows], prims[1, rows], prims[2, rows])
        star[pl.ds(block * Y_FACES, Y_FACES)] = s
        speed[pl.ds(block * Y_FACES, Y_FACES)] = u

    @pl.loop(0, 32 // Y_CELLS)
    def _(block):
        first = block * Y_CELLS
        rows = pl.ds(first + HALO - 1, Y_CELLS + 2)
        near = pl.ds(first, Y_CELLS + 3)
        new = remap([fields[index, rows] for index in range(5)], 2, star[near], speed[near], step)
        for index in range(5):
            out[pl.ds(block * (Y_CELLS // 2), Y_CELLS // 2), 2 * index : 2 * index + 2] = new[index].reshape(
                Y_CELLS // 2, 2, LINES, LANES
            )


Z_FACES = 8


def column_kernel(top, lines, out, prims, star, speed):
    step = step_of(top)

    @pl.loop(0, 2)
    def _(row):
        fields = [lines[:, 2 * index + row] for index in range(5)]
        along, press, half_reach = primitives(fields[0], fields[1:4], fields[4], 2, step)
        for index, value in enumerate((fields[0], along, press, half_reach)):
            prims[index, 2:18] = value
            prims[index, 0:2] = value[14:16]
            prims[index, 18:21] = value[0:3]

        @pl.loop(0, 16 // Z_FACES)
        def _(block):
            cells = pl.ds(block * Z_FACES, Z_FACES + 5)
            s, u = interfaces(*(prims[index, cells] for index in range(4)))
            star[pl.ds(block * Z_FACES, Z_FACES)] = s
            speed[pl.ds(block * Z_FACES, Z_FACES)] = u

        def ring(value, before, after):
            return jnp.concatenate([value[16 - before :], value, value[:after]], axis=0)

        new = remap(
            [ring(f, 1, 1) for f in fields], 3, ring(star[...], 2, 1), ring(speed[...], 2, 1), step
        )
        for index in range(5):
            for z in range(16):
                out[index, z, pl.ds(row, LINES, stride=2), :] = new[index][z]


def tiled(array):
    lead = array.shape[:-2]
    split = array.reshape(lead + (4, LINES, LINES, LANES))
    return jnp.swapaxes(split, -3, -2).reshape(lead + (256, LANES))


def swap_speeds(speeds, axes):
    devices = speeds.shape[0]
    swapped = lax.all_to_all(speeds.reshape(devices, 1, LANES), axes, split_axis=0, concat_axis=0, tiled=True)
    return swapped.reshape(devices, LANES)


def local(density, velocity, pressure, sizes):
    vmem = pl.BlockSpec(memory_space=pltpu.VMEM)
    density = tiled(density[0])
    velocity = tiled(velocity[:, 0])
    pressure = tiled(pressure[0])
    near = sizes["x"] * sizes["core"]
    far = sizes["y_hi"] * sizes["z"] * sizes["y_lo"]
    rows = sizes["y_hi"] * sizes["z"]
    halo = jax.ShapeDtypeStruct((5, HALO, LINES, LANES), F32)
    fastest, low, high = pl.pallas_call(
        survey_kernel,
        out_shape=(jax.ShapeDtypeStruct((near, LANES), F32), halo, halo),
        in_specs=[vmem] * 3,
        out_specs=(vmem, vmem, vmem),
        name="survey",
    )(density, velocity, pressure)
    below = lax.ppermute(high, ROW, [(i, (i + 1) % rows) for i in range(rows)])
    above = lax.ppermute(low, ROW, [(i, (i - 1) % rows) for i in range(rows)])
    fastest = pl.pallas_call(
        gather_kernel,
        out_shape=jax.ShapeDtypeStruct((far, LANES), F32),
        in_specs=[vmem],
        out_specs=vmem,
        name="gather_speeds",
    )(swap_speeds(fastest, ("x", "core")))
    top = swap_speeds(fastest, ("y_hi", "z", "y_lo"))
    lines = pl.pallas_call(
        plane_kernel,
        out_shape=jax.ShapeDtypeStruct((16, 10, LINES, LANES), F32),
        in_specs=[vmem] * 6,
        out_specs=vmem,
        scratch_shapes=[
            pltpu.VMEM((5, 40, LINES, LANES), F32),
            pltpu.VMEM((5, 40, LINES, LANES), F32),
            pltpu.VMEM((3, 40, LINES, LANES), F32),
            pltpu.VMEM((35, LINES, LANES), F32),
            pltpu.VMEM((35, LINES, LANES), F32),
        ],
        compiler_params=pltpu.CompilerParams(vmem_limit_bytes=32 * 1024 * 1024),
        name="plane_sweeps",
    )(top, density, velocity, pressure, below, above)
    lines = lax.all_to_all(lines, COL, split_axis=0, concat_axis=0, tiled=True)
    result = pl.pallas_call(
        column_kernel,
        out_shape=jax.ShapeDtypeStruct((5, 16, 16, LANES), F32),
        in_specs=[vmem, vmem],
        out_specs=vmem,
        scratch_shapes=[
            pltpu.VMEM((4, 21, LINES, LANES), F32),
            pltpu.VMEM((16, LINES, LANES), F32),
            pltpu.VMEM((16, LINES, LANES), F32),
        ],
        compiler_params=pltpu.CompilerParams(vmem_limit_bytes=32 * 1024 * 1024),
        name="column_sweep",
    )(top, lines)
    return jnp.swapaxes(result.reshape(5, 16, LINES, 2, LANES), 2, 3).reshape(5, 16, 2, LINES * LANES)


ROW = ("y_hi", "z")
COL = ("y_lo", "x", "core")


def solution(mesh):
    rows, cols = mesh.shape["row"], mesh.shape["col"]
    sizes = {"y_hi": 4, "z": rows // 4, "y_lo": 2, "x": cols // 4, "core": 2}
    parts = jax.sharding.Mesh(mesh.devices.reshape(tuple(sizes.values())), ROW + COL)
    placed = (P(COL, ROW, None), P(None, COL, ROW, None), P(COL, ROW, None))

    def step(density, velocity, pressure):
        return local(density, velocity, pressure, sizes)

    return jax.shard_map(
        step,
        mesh=parts,
        in_specs=placed,
        out_specs=P(None, None, ROW + COL, None),
        check_vma=False,
    )
```

```python
import jax
import jax.numpy as jnp
from jax import lax
from jax.experimental import pallas as pl
from jax.experimental.pallas import tpu as pltpu
from jax.sharding import PartitionSpec as P

RITER = 5
ADIABATIC = 5.0 / 3.0
COURANT_NUMBER = 0.3
PRESSURE_FLOOR = 0.05

LINES = 8
LANES = 128
HALO = 4
ROWS = 32
DEPTH = 16
F32 = jnp.float32


def inverse(value):
    return pl.reciprocal(value, approx=False)


def root(value):
    return value * lax.rsqrt(value)


def faces(before, here, after, beyond):
    value = 7.0 / 12.0 * (here + after) - 1.0 / 12.0 * (before + beyond)
    return jnp.minimum(jnp.maximum(value, jnp.minimum(here, after)), jnp.maximum(here, after))


def parabola(here, lower, upper):
    rise, fall = here - lower, upper - here
    return rise + fall, rise - fall


def reaches(half_reach):
    return half_reach, 3.0 * half_reach - 4.0 * half_reach * half_reach


def riemann(mass_l, speed_l, press_l, mass_r, speed_r, press_r):
    mass_l, mass_r = jnp.maximum(mass_l, PRESSURE_FLOOR), jnp.maximum(mass_r, PRESSURE_FLOOR)
    press_l, press_r = jnp.maximum(press_l, PRESSURE_FLOOR), jnp.maximum(press_r, PRESSURE_FLOOR)
    gain_l = (ADIABATIC + 1.0) / ADIABATIC * inverse(press_l)
    gain_r = (ADIABATIC + 1.0) / ADIABATIC * inverse(press_r)
    light_l = lax.rsqrt(0.5 * ADIABATIC * press_l * mass_l)
    light_r = lax.rsqrt(0.5 * ADIABATIC * press_r * mass_r)
    rest = (ADIABATIC - 1.0) / ADIABATIC
    closing = speed_l - speed_r
    star = (press_l * light_l + press_r * light_r + 2.0**0.5 * closing) * inverse(light_l + light_r)
    star = jnp.maximum(star, PRESSURE_FLOOR)
    for _ in range(RITER):
        root_l = lax.rsqrt(gain_l * star + rest)
        root_r = lax.rsqrt(gain_r * star + rest)
        slow_l = root_l * light_l
        slow_r = root_r * light_r
        gap = closing - (star - press_l) * slow_l - (star - press_r) * slow_r
        bottom = slow_l * (root_l * root_l + 0.5) + slow_r * (root_r * root_r + 0.5)
        star = jnp.maximum(star + gap * inverse(bottom), PRESSURE_FLOOR)
    slow_l = lax.rsqrt(gain_l * star + rest) * light_l
    slow_r = lax.rsqrt(gain_r * star + rest) * light_r
    speed = speed_l * slow_r + speed_r * slow_l + (press_l - press_r) * (slow_l * slow_r)
    return star, speed * inverse(slow_l + slow_r)


def primitives(mass, moments, energy, normal, step):
    thin = inverse(mass)
    square = moments[0] * moments[0] + moments[1] * moments[1] + moments[2] * moments[2]
    press = jnp.maximum((ADIABATIC - 1.0) * (energy - 0.5 * square * thin), PRESSURE_FLOOR)
    return moments[normal] * thin, press, 0.5 * step * root(ADIABATIC * press * thin)


def interfaces(mass, speed, press, half_reach):
    n = mass.shape[0] - 5
    half, bent = reaches(half_reach[2 : n + 3])
    sides = []
    for value in (mass, speed, press):
        face = faces(value[: n + 2], value[1 : n + 3], value[2 : n + 4], value[3 : n + 5])
        lower, upper = face[: n + 1], face[1:]
        slope, curve = parabola(value[2 : n + 3], lower, upper)
        slope, curve = half * slope, bent * curve
        sides.append(((upper - slope + curve)[:n], (lower + slope + curve)[1:]))
    (mass_l, mass_r), (speed_l, speed_r), (press_l, press_r) = sides
    return riemann(mass_l, speed_l, press_l, mass_r, speed_r, press_r)


def remap(fields, normal, star, speed, step):
    n = star.shape[0] - 3
    shift = step * speed
    work = shift * star
    push = step * star
    thin = inverse(1.0 + (shift[1:] - shift[:-1]))
    amounts = list(fields)
    amounts[normal] = fields[normal] - (push[1:] - push[:-1])
    amounts[4] = fields[4] - (work[1:] - work[:-1])
    ahead = jnp.maximum(shift[1:-1], 0.0) * thin[:-1]
    back = jnp.minimum(shift[1:-1], 0.0) * thin[1:]
    keep = 1.0 - ahead[1:] + back[:-1]
    return [a[1 : n + 1] * keep + a[:n] * ahead[:-1] - a[2:] * back[1:] for a in amounts]


def shift_up(value):
    lane = lax.broadcasted_iota(jnp.int32, value.shape, 2)
    turned = pltpu.roll(value, LANES - 1, 2)
    groups = turned.reshape(-1, LINES, LINES, LANES)
    after = jnp.concatenate([groups[:, 1:], groups[:, :1]], axis=1).reshape(value.shape)
    return jnp.where(lane == LANES - 1, after, turned)


def shift_down(value):
    lane = lax.broadcasted_iota(jnp.int32, value.shape, 2)
    turned = pltpu.roll(value, 1, 2)
    groups = turned.reshape(-1, LINES, LINES, LANES)
    before = jnp.concatenate([groups[:, LINES - 1 :], groups[:, : LINES - 1]], axis=1).reshape(value.shape)
    return jnp.where(lane == 0, before, turned)


def prepare(mass, speeds, press):
    press = jnp.maximum(press, PRESSURE_FLOOR)
    square = speeds[0] * speeds[0] + speeds[1] * speeds[1] + speeds[2] * speeds[2]
    energy = 1.0 / (ADIABATIC - 1.0) * press + 0.5 * mass * square
    sound = root(ADIABATIC * press * inverse(mass))
    held = [mass, mass * speeds[0], mass * speeds[1], mass * speeds[2], energy, sound]
    for value in (mass, speeds[0], press):
        after = shift_up(value)
        face = faces(shift_down(value), value, after, shift_up(after))
        held.extend((face,) + parabola(value, shift_down(face), face))
    return held


def solve_x(sound, shapes, step):
    half, bent = reaches(0.5 * step * sound)
    sides = []
    for face, slope, curve in shapes:
        lower = face - slope
        slope, curve = half * slope, bent * curve
        sides.append((face - slope + curve, shift_up(lower + slope + curve)))
    (mass_l, mass_r), (speed_l, speed_r), (press_l, press_r) = sides
    return riemann(mass_l, speed_l, press_l, mass_r, speed_r, press_r)


def remap_x(fields, star, speed, step):
    shift = step * speed
    shift_low, star_low = shift_down(shift), shift_down(star)
    thin = inverse(1.0 + (shift - shift_low))
    amounts = list(fields)
    amounts[1] = fields[1] - step * (star - star_low)
    amounts[4] = fields[4] - (shift * star - shift_low * star_low)
    ahead = jnp.maximum(shift, 0.0) * thin
    back = jnp.minimum(shift, 0.0) * shift_up(thin)
    flux = [ahead * a + back * shift_up(a) for a in amounts]
    return [a - f + shift_down(f) for a, f in zip(amounts, flux)]


def survey_kernel(odd, density, velocity, pressure, speed, paired, other):
    mass, press = density[...], pressure[...]
    sound = ADIABATIC * press / mass
    largest = jnp.maximum(jnp.abs(velocity[0]), jnp.abs(velocity[1]))
    largest = jnp.maximum(largest, jnp.abs(velocity[2])) + root(sound)
    speed[...] = jnp.full(speed.shape, jnp.max(largest), F32)
    refs = (density, velocity.at[0], velocity.at[1], velocity.at[2], pressure)
    for index, ref in enumerate(refs):
        for tile in range(LINES):
            low = ref[pl.ds(tile * LINES, HALO), :]
            high = ref[pl.ds((ROWS - LINES + tile) * LINES + HALO, HALO), :]
            paired[index, tile] = jnp.where(odd[0, 0] == 1, low, high)
            other[0, index, tile] = low
            other[1, index, tile] = high


def step_of(speeds):
    return COURANT_NUMBER / jnp.broadcast_to(jnp.max(speeds[...], axis=0, keepdims=True), (LINES, LANES))


def blocks(total, size):
    return [slice(first, min(first + size, total)) for first in range(0, total, size)]


HELD = 15
Y_FACES = 35
Y_CELLS = 32


def to_lines(ref, tiles, rows):
    for place in range(tiles.shape[0]):
        group, line = rows.start // LINES + place // LINES, place % LINES
        if group < ROWS // LINES:
            ref[pl.ds((group * LINES + HALO) * LINES + line, LINES, stride=LINES), :] = tiles[place]
        else:
            ref[pl.ds(line, HALO, stride=LINES), :] = tiles[place, :HALO]
            ref[pl.ds((ROWS + HALO) * LINES + line, HALO, stride=LINES), :] = tiles[place, HALO:]


def sweep_x(fields, step):
    held = prepare(fields[0], fields[1:4], fields[4])
    star, speed = solve_x(held[5], (held[6:9], held[9:12], held[12:15]), step)
    new = remap_x(held[:5], star, speed, step)
    return new + list(primitives(new[0], new[1:4], new[4], 1, step))


def lines_of(ref, index, rows):
    return ref[index, rows.start * LINES : rows.stop * LINES].reshape(-1, LINES, LANES)


def sweep_y(lines, out, star, speed, step):
    for part in blocks(ROWS + 3, Y_FACES):
        rows = slice(part.start, part.stop + 5)
        star[part], speed[part] = interfaces(*(lines_of(lines, index, rows) for index in (0, 5, 6, 7)))
    for cells in blocks(ROWS, Y_CELLS):
        rows = slice(cells.start + HALO - 1, cells.stop + HALO + 1)
        near = slice(cells.start, cells.stop + 3)
        new = remap([lines_of(lines, index, rows) for index in range(5)], 2, star[near], speed[near], step)
        for index in range(5):
            pairs = new[index].reshape(-1, 2, LINES, LANES)
            out[cells.start // 2 : cells.stop // 2, 2 * index : 2 * index + 2] = pairs


def raw_tiles(density, velocity, pressure):
    refs = (density, velocity.at[0], velocity.at[1], velocity.at[2], pressure)
    return [ref[...].reshape(-1, LINES, LANES) for ref in refs]


def plane_kernel(odd, top, density, velocity, pressure, paired, other, out, rim, lines, star, speed):
    step = step_of(top)
    for index in range(5):
        rim[index, :, :HALO] = jnp.where(odd[0, 0] == 1, paired[index], other[1, index])
        rim[index, :, HALO:] = jnp.where(odd[0, 0] == 1, other[0, index], paired[index])
    inner = raw_tiles(density, velocity, pressure)
    swept = sweep_x([jnp.concatenate([inner[index], rim[index]], axis=0) for index in range(5)], step)
    for index in range(8):
        to_lines(lines.at[index], swept[index], slice(0, ROWS + 2 * HALO))
    sweep_y(lines, out, star, speed, step)


def column_kernel(top, lines, out):
    step = step_of(top)
    for row in range(2):
        fields = [lines[:, 2 * index + row] for index in range(5)]
        along, press, half_reach = primitives(fields[0], fields[1:4], fields[4], 2, step)

        def ring(value, before, after):
            return jnp.concatenate([value[DEPTH - before :], value, value[:after]], axis=0)

        star_now, speed_now = interfaces(*(ring(value, 2, 3) for value in (fields[0], along, press, half_reach)))
        new = remap([ring(f, 1, 1) for f in fields], 3, ring(star_now, 2, 1), ring(speed_now, 2, 1), step)
        for index in range(5):
            for z in range(DEPTH):
                out[index, z, pl.ds(row, LINES, stride=2), :] = new[index][z]


def tiled(array):
    lead = array.shape[:-2]
    split = array.reshape(lead + (ROWS // LINES, LINES, LINES, LANES))
    return jnp.swapaxes(split, -3, -2).reshape(lead + (ROWS * LINES, LANES))


def swap_speeds(speeds, axes):
    order = list(range(speeds.shape[0]))[::-1]
    swapped = lax.all_to_all(speeds, axes, split_axis=0, concat_axis=0, tiled=True, axis_index_groups=[order])
    return swapped.reshape(-1, LANES)


def local(density, velocity, pressure, sizes):
    vmem = pl.BlockSpec(memory_space=pltpu.VMEM)
    smem = pl.BlockSpec(memory_space=pltpu.SMEM)
    wide = pltpu.CompilerParams(vmem_limit_bytes=32 * 1024 * 1024)
    density = tiled(density[0])
    velocity = tiled(velocity[:, 0])
    pressure = tiled(pressure[0])
    near = sizes["x"] * sizes["core"]
    far = sizes["y_hi"] * sizes["z"] * sizes["y_lo"]
    rows = sizes["y_hi"] * sizes["z"]
    halo = jax.ShapeDtypeStruct((5, LINES, HALO, LANES), F32)
    both = jax.ShapeDtypeStruct((2, 5, LINES, HALO, LANES), F32)
    odd = (lax.axis_index("z") % 2).reshape(1, 1)
    fastest, paired, other = pl.pallas_call(
        survey_kernel,
        out_shape=(jax.ShapeDtypeStruct((near * 16, LANES), F32), halo, both),
        in_specs=[smem] + [vmem] * 3,
        out_specs=(vmem, vmem, vmem),
        name="survey",
    )(odd, density, velocity, pressure)
    other = lax.ppermute(other, ROW, [(i, (i + i % 2 * 2 - 1) % rows) for i in range(rows)])
    fastest = swap_speeds(fastest.reshape(near, 16, LANES), ("x", "core"))
    fastest = jnp.broadcast_to(jnp.max(fastest, axis=0, keepdims=True), (far, 2, LANES))
    fastest, paired = lax.optimization_barrier((fastest, paired))
    top = swap_speeds(fastest, ("y_hi", "z", "y_lo"))
    paired = lax.ppermute(paired, ROW, [(i, i ^ 1) for i in range(rows)])
    faces_shape = pltpu.VMEM((ROWS + 3, LINES, LANES), F32)
    rim_shape = pltpu.VMEM((5, LINES, LINES, LANES), F32)
    lines_shape = (8, (ROWS + 2 * HALO) * LINES, LANES)
    sent_shape = jax.ShapeDtypeStruct((DEPTH, 10, LINES, LANES), F32)
    lines = pl.pallas_call(
        plane_kernel,
        out_shape=sent_shape,
        in_specs=[smem] + [vmem] * 6,
        out_specs=vmem,
        scratch_shapes=[rim_shape, pltpu.VMEM(lines_shape, F32), faces_shape, faces_shape],
        compiler_params=wide,
        name="plane_sweeps",
    )(odd, top, density, velocity, pressure, paired, other)
    lines = lax.all_to_all(lines, COL, split_axis=0, concat_axis=0, tiled=True)
    result = pl.pallas_call(
        column_kernel,
        out_shape=jax.ShapeDtypeStruct((5, DEPTH, 2 * LINES, LANES), F32),
        in_specs=[vmem, vmem],
        out_specs=vmem,
        compiler_params=wide,
        name="column_sweep",
    )(top, lines)
    return jnp.swapaxes(result.reshape(5, DEPTH, LINES, 2, LANES), 2, 3).reshape(5, DEPTH, 2, LINES * LANES)


ROW = ("y_hi", "z")
COL = ("y_lo", "x", "core")


def solution(mesh):
    rows, cols = mesh.shape["row"], mesh.shape["col"]
    sizes = {"y_hi": 4, "z": rows // 4, "y_lo": 2, "x": cols // 4, "core": 2}
    parts = jax.sharding.Mesh(mesh.devices.reshape(tuple(sizes.values())), ROW + COL)
    placed = (P(COL, ROW, None), P(None, COL, ROW, None), P(COL, ROW, None))

    def step(density, velocity, pressure):
        return local(density, velocity, pressure, sizes)

    return jax.shard_map(
        step,
        mesh=parts,
        in_specs=placed,
        out_specs=P(None, None, ROW + COL, None),
        check_vma=False,
    )
```

```python
import jax
import jax.numpy as jnp
from jax import lax
from jax.experimental import pallas as pl
from jax.experimental.pallas import tpu as pltpu
from jax.sharding import PartitionSpec as P

RITER = 5
ADIABATIC = 5.0 / 3.0
COURANT_NUMBER = 0.3
PRESSURE_FLOOR = 0.05

LINES = 8
LANES = 128
HALO = 4
ROWS = 32
DEPTH = 16
F32 = jnp.float32


def inverse(value):
    return pl.reciprocal(value, approx=False)


def root(value):
    return value * lax.rsqrt(value)


def faces(before, here, after, beyond):
    value = 7.0 / 12.0 * (here + after) - 1.0 / 12.0 * (before + beyond)
    return jnp.minimum(jnp.maximum(value, jnp.minimum(here, after)), jnp.maximum(here, after))


def parabola(here, lower, upper):
    rise, fall = here - lower, upper - here
    return rise + fall, rise - fall


def reaches(half_reach):
    return half_reach, 3.0 * half_reach - 4.0 * half_reach * half_reach


def riemann(mass_l, speed_l, press_l, mass_r, speed_r, press_r):
    mass_l, mass_r = jnp.maximum(mass_l, PRESSURE_FLOOR), jnp.maximum(mass_r, PRESSURE_FLOOR)
    press_l, press_r = jnp.maximum(press_l, PRESSURE_FLOOR), jnp.maximum(press_r, PRESSURE_FLOOR)
    gain_l = (ADIABATIC + 1.0) / ADIABATIC * inverse(press_l)
    gain_r = (ADIABATIC + 1.0) / ADIABATIC * inverse(press_r)
    light_l = lax.rsqrt(0.5 * ADIABATIC * press_l * mass_l)
    light_r = lax.rsqrt(0.5 * ADIABATIC * press_r * mass_r)
    rest = (ADIABATIC - 1.0) / ADIABATIC
    closing = speed_l - speed_r
    star = (press_l * light_l + press_r * light_r + 2.0**0.5 * closing) * inverse(light_l + light_r)
    star = jnp.maximum(star, PRESSURE_FLOOR)
    for _ in range(RITER):
        root_l = lax.rsqrt(gain_l * star + rest)
        root_r = lax.rsqrt(gain_r * star + rest)
        slow_l = root_l * light_l
        slow_r = root_r * light_r
        gap = closing - (star - press_l) * slow_l - (star - press_r) * slow_r
        bottom = slow_l * (root_l * root_l + 0.5) + slow_r * (root_r * root_r + 0.5)
        star = jnp.maximum(star + gap * inverse(bottom), PRESSURE_FLOOR)
    slow_l = lax.rsqrt(gain_l * star + rest) * light_l
    slow_r = lax.rsqrt(gain_r * star + rest) * light_r
    speed = speed_l * slow_r + speed_r * slow_l + (press_l - press_r) * (slow_l * slow_r)
    return star, speed * inverse(slow_l + slow_r)


def primitives(mass, moments, energy, normal, step):
    thin = inverse(mass)
    square = moments[0] * moments[0] + moments[1] * moments[1] + moments[2] * moments[2]
    press = jnp.maximum((ADIABATIC - 1.0) * (energy - 0.5 * square * thin), PRESSURE_FLOOR)
    return moments[normal] * thin, press, 0.5 * step * root(ADIABATIC * press * thin)


def interfaces(mass, speed, press, half_reach):
    n = mass.shape[0] - 5
    half, bent = reaches(half_reach[2 : n + 3])
    sides = []
    for value in (mass, speed, press):
        face = faces(value[: n + 2], value[1 : n + 3], value[2 : n + 4], value[3 : n + 5])
        lower, upper = face[: n + 1], face[1:]
        slope, curve = parabola(value[2 : n + 3], lower, upper)
        slope, curve = half * slope, bent * curve
        sides.append(((upper - slope + curve)[:n], (lower + slope + curve)[1:]))
    (mass_l, mass_r), (speed_l, speed_r), (press_l, press_r) = sides
    return riemann(mass_l, speed_l, press_l, mass_r, speed_r, press_r)


def remap(fields, normal, star, speed, step):
    n = star.shape[0] - 3
    shift = step * speed
    work = shift * star
    push = step * star
    thin = inverse(1.0 + (shift[1:] - shift[:-1]))
    amounts = list(fields)
    amounts[normal] = fields[normal] - (push[1:] - push[:-1])
    amounts[4] = fields[4] - (work[1:] - work[:-1])
    ahead = jnp.maximum(shift[1:-1], 0.0) * thin[:-1]
    back = jnp.minimum(shift[1:-1], 0.0) * thin[1:]
    keep = 1.0 - ahead[1:] + back[:-1]
    return [a[1 : n + 1] * keep + a[:n] * ahead[:-1] - a[2:] * back[1:] for a in amounts]


def shift_up(value):
    lane = lax.broadcasted_iota(jnp.int32, value.shape, 2)
    turned = pltpu.roll(value, LANES - 1, 2)
    groups = turned.reshape(-1, LINES, LINES, LANES)
    after = jnp.concatenate([groups[:, 1:], groups[:, :1]], axis=1).reshape(value.shape)
    return jnp.where(lane == LANES - 1, after, turned)


def shift_down(value):
    lane = lax.broadcasted_iota(jnp.int32, value.shape, 2)
    turned = pltpu.roll(value, 1, 2)
    groups = turned.reshape(-1, LINES, LINES, LANES)
    before = jnp.concatenate([groups[:, LINES - 1 :], groups[:, : LINES - 1]], axis=1).reshape(value.shape)
    return jnp.where(lane == 0, before, turned)


def prepare(mass, speeds, press):
    press = jnp.maximum(press, PRESSURE_FLOOR)
    square = speeds[0] * speeds[0] + speeds[1] * speeds[1] + speeds[2] * speeds[2]
    energy = 1.0 / (ADIABATIC - 1.0) * press + 0.5 * mass * square
    sound = root(ADIABATIC * press * inverse(mass))
    held = [mass, mass * speeds[0], mass * speeds[1], mass * speeds[2], energy, sound]
    for value in (mass, speeds[0], press):
        after = shift_up(value)
        face = faces(shift_down(value), value, after, shift_up(after))
        held.extend((face,) + parabola(value, shift_down(face), face))
    return held


def solve_x(sound, shapes, step):
    half, bent = reaches(0.5 * step * sound)
    sides = []
    for face, slope, curve in shapes:
        lower = face - slope
        slope, curve = half * slope, bent * curve
        sides.append((face - slope + curve, shift_up(lower + slope + curve)))
    (mass_l, mass_r), (speed_l, speed_r), (press_l, press_r) = sides
    return riemann(mass_l, speed_l, press_l, mass_r, speed_r, press_r)


def remap_x(fields, star, speed, step):
    shift = step * speed
    shift_low, star_low = shift_down(shift), shift_down(star)
    thin = inverse(1.0 + (shift - shift_low))
    amounts = list(fields)
    amounts[1] = fields[1] - step * (star - star_low)
    amounts[4] = fields[4] - (shift * star - shift_low * star_low)
    ahead = jnp.maximum(shift, 0.0) * thin
    back = jnp.minimum(shift, 0.0) * shift_up(thin)
    flux = [ahead * a + back * shift_up(a) for a in amounts]
    return [a - f + shift_down(f) for a, f in zip(amounts, flux)]


def survey_kernel(odd, density, velocity, pressure, speed, paired, other):
    mass, press = density[...], pressure[...]
    sound = ADIABATIC * press / mass
    largest = jnp.maximum(jnp.abs(velocity[0]), jnp.abs(velocity[1]))
    largest = jnp.maximum(largest, jnp.abs(velocity[2])) + root(sound)
    speed[...] = jnp.full(speed.shape, jnp.max(largest), F32)
    refs = (density, velocity.at[0], velocity.at[1], velocity.at[2], pressure)
    for index, ref in enumerate(refs):
        for tile in range(LINES):
            low = ref[pl.ds(tile * LINES, HALO), :]
            high = ref[pl.ds((ROWS - LINES + tile) * LINES + HALO, HALO), :]
            paired[index, tile] = jnp.where(odd[0, 0] == 1, low, high)
            other[0, index, tile] = low
            other[1, index, tile] = high


def step_of(speeds):
    return COURANT_NUMBER / jnp.broadcast_to(jnp.max(speeds[...], axis=0, keepdims=True), (LINES, LANES))


def blocks(total, size):
    return [slice(first, min(first + size, total)) for first in range(0, total, size)]


HELD = 15
Y_FACES = 35
Y_CELLS = 32


def to_lines(ref, tiles, rows):
    for place in range(tiles.shape[0]):
        group, line = rows.start // LINES + place // LINES, place % LINES
        if group < ROWS // LINES:
            ref[pl.ds((group * LINES + HALO) * LINES + line, LINES, stride=LINES), :] = tiles[place]
        else:
            ref[pl.ds(line, HALO, stride=LINES), :] = tiles[place, :HALO]
            ref[pl.ds((ROWS + HALO) * LINES + line, HALO, stride=LINES), :] = tiles[place, HALO:]


def sweep_x(held, step):
    star, speed = solve_x(held[5], (held[6:9], held[9:12], held[12:15]), step)
    new = remap_x(held[:5], star, speed, step)
    return new + list(primitives(new[0], new[1:4], new[4], 1, step))


def seat(column):
    return column ^ 4


def lines_of(ref, index, rows):
    return ref[index, rows.start * LINES : rows.stop * LINES].reshape(-1, LINES, LANES)


def sweep_y(lines, out, star, speed, step):
    for part in blocks(ROWS + 3, Y_FACES):
        rows = slice(part.start, part.stop + 5)
        star[part], speed[part] = interfaces(*(lines_of(lines, index, rows) for index in (0, 5, 6, 7)))
    for cells in blocks(ROWS, Y_CELLS):
        rows = slice(cells.start + HALO - 1, cells.stop + HALO + 1)
        near = slice(cells.start, cells.stop + 3)
        new = remap([lines_of(lines, index, rows) for index in range(5)], 2, star[near], speed[near], step)
        for index in range(5):
            pairs = new[index].reshape(-1, 2, LINES, LANES)
            for pair in range(pairs.shape[0]):
                out[seat(cells.start // 2 + pair), 2 * index : 2 * index + 2] = pairs[pair]


def raw_tiles(density, velocity, pressure):
    refs = (density, velocity.at[0], velocity.at[1], velocity.at[2], pressure)
    return [ref[...].reshape(-1, LINES, LANES) for ref in refs]


def prepare_kernel(density, velocity, pressure, held):
    inner = raw_tiles(density, velocity, pressure)
    for index, value in enumerate(prepare(inner[0], inner[1:4], inner[4])):
        held[index] = value


def plane_kernel(odd, top, held, paired, other, out, rim, lines, star, speed):
    step = step_of(top)
    for index in range(5):
        rim[index, :, :HALO] = jnp.where(odd[0, 0] == 1, paired[index], other[1, index])
        rim[index, :, HALO:] = jnp.where(odd[0, 0] == 1, other[0, index], paired[index])
    outer = prepare(rim[0], [rim[1], rim[2], rim[3]], rim[4])
    swept = sweep_x([jnp.concatenate([held[index], outer[index]], axis=0) for index in range(HELD)], step)
    for index in range(8):
        to_lines(lines.at[index], swept[index], slice(0, ROWS + 2 * HALO))
    sweep_y(lines, out, star, speed, step)


def column_kernel(top, lines, out):
    step = step_of(top)
    for row in range(2):
        fields = [jnp.stack([lines[seat(z), 2 * index + row] for z in range(DEPTH)]) for index in range(5)]
        along, press, half_reach = primitives(fields[0], fields[1:4], fields[4], 2, step)

        def ring(value, before, after):
            return jnp.concatenate([value[DEPTH - before :], value, value[:after]], axis=0)

        star_now, speed_now = interfaces(*(ring(value, 2, 3) for value in (fields[0], along, press, half_reach)))
        new = remap([ring(f, 1, 1) for f in fields], 3, ring(star_now, 2, 1), ring(speed_now, 2, 1), step)
        for index in range(5):
            for z in range(DEPTH):
                out[index, z, pl.ds(row, LINES, stride=2), :] = new[index][z]


def tiled(array):
    lead = array.shape[:-2]
    split = array.reshape(lead + (ROWS // LINES, LINES, LINES, LANES))
    return jnp.swapaxes(split, -3, -2).reshape(lead + (ROWS * LINES, LANES))


def swap_speeds(speeds, axes):
    order = list(range(speeds.shape[0]))[::-1]
    swapped = lax.all_to_all(speeds, axes, split_axis=0, concat_axis=0, tiled=True, axis_index_groups=[order])
    return swapped.reshape(-1, LANES)


def local(density, velocity, pressure, sizes):
    vmem = pl.BlockSpec(memory_space=pltpu.VMEM)
    smem = pl.BlockSpec(memory_space=pltpu.SMEM)
    wide = pltpu.CompilerParams(vmem_limit_bytes=32 * 1024 * 1024)
    density = tiled(density[0])
    velocity = tiled(velocity[:, 0])
    pressure = tiled(pressure[0])
    near = sizes["x"] * sizes["core"]
    far = sizes["y_hi"] * sizes["z"] * sizes["y_lo"]
    rows = sizes["y_hi"] * sizes["z"]
    halo = jax.ShapeDtypeStruct((5, LINES, HALO, LANES), F32)
    both = jax.ShapeDtypeStruct((2, 5, LINES, HALO, LANES), F32)
    odd = (lax.axis_index("z") & 1).reshape(1, 1)
    fastest, paired, other = pl.pallas_call(
        survey_kernel,
        out_shape=(jax.ShapeDtypeStruct((near * 16, LANES), F32), halo, both),
        in_specs=[smem] + [vmem] * 3,
        out_specs=(vmem, vmem, vmem),
        name="survey",
    )(odd, density, velocity, pressure)
    other = lax.ppermute(other, ROW, [(i, (i + i % 2 * 2 - 1) % rows) for i in range(rows)])
    fastest = swap_speeds(fastest.reshape(near, 16, LANES), ("x", "core"))
    fastest = jnp.broadcast_to(jnp.max(fastest, axis=0, keepdims=True), (far, 2, LANES))
    fastest, paired, density, velocity, pressure = lax.optimization_barrier((fastest, paired, density, velocity, pressure))
    top = swap_speeds(fastest, ("y_hi", "z", "y_lo"))
    paired = lax.ppermute(paired, ROW, [(i, i ^ 1) for i in range(rows)])
    held = pl.pallas_call(
        prepare_kernel,
        out_shape=jax.ShapeDtypeStruct((HELD, ROWS, LINES, LANES), F32),
        in_specs=[vmem] * 3,
        out_specs=vmem,
        compiler_params=pltpu.CompilerParams(vmem_limit_bytes=32 * 1024 * 1024),
        cost_estimate=pl.CostEstimate(flops=4000000, bytes_accessed=2600000, transcendentals=100000),
        name="prepare_rows",
    )(density, velocity, pressure)
    faces_shape = pltpu.VMEM((ROWS + 3, LINES, LANES), F32)
    rim_shape = pltpu.VMEM((5, LINES, LINES, LANES), F32)
    lines_shape = (8, (ROWS + 2 * HALO) * LINES, LANES)
    sent_shape = jax.ShapeDtypeStruct((DEPTH, 10, LINES, LANES), F32)
    lines = pl.pallas_call(
        plane_kernel,
        out_shape=sent_shape,
        in_specs=[smem] + [vmem] * 4,
        out_specs=vmem,
        scratch_shapes=[rim_shape, pltpu.VMEM(lines_shape, F32), faces_shape, faces_shape],
        compiler_params=wide,
        name="plane_sweeps",
    )(odd, top, held, paired, other)
    seats = [seat(column) for column in range(DEPTH)]
    lines = lax.all_to_all(lines, COL, split_axis=0, concat_axis=0, tiled=True, axis_index_groups=[seats])
    result = pl.pallas_call(
        column_kernel,
        out_shape=jax.ShapeDtypeStruct((5, DEPTH, 2 * LINES, LANES), F32),
        in_specs=[vmem, vmem],
        out_specs=vmem,
        compiler_params=wide,
        name="column_sweep",
    )(top, lines)
    return jnp.swapaxes(result.reshape(5, DEPTH, LINES, 2, LANES), 2, 3).reshape(5, DEPTH, 2, LINES * LANES)


ROW = ("y_hi", "z")
COL = ("y_lo", "x", "core")


def solution(mesh):
    rows, cols = mesh.shape["row"], mesh.shape["col"]
    sizes = {"y_hi": 4, "z": rows // 4, "y_lo": 2, "x": cols // 4, "core": 2}
    parts = jax.sharding.Mesh(mesh.devices.reshape(tuple(sizes.values())), ROW + COL)
    placed = (P(COL, ROW, None), P(None, COL, ROW, None), P(COL, ROW, None))

    def step(density, velocity, pressure):
        return local(density, velocity, pressure, sizes)

    return jax.shard_map(
        step,
        mesh=parts,
        in_specs=placed,
        out_specs=P(None, None, ROW + COL, None),
        check_vma=False,
    )
```

```python
import jax
import jax.numpy as jnp
from jax import lax
from jax.experimental import pallas as pl
from jax.experimental.pallas import tpu as pltpu
from jax.sharding import PartitionSpec as P

RITER = 5
ADIABATIC = 5.0 / 3.0
COURANT_NUMBER = 0.3
PRESSURE_FLOOR = 0.05

LINES = 8
LANES = 128
HALO = 4
ROWS = 32
DEPTH = 16
F32 = jnp.float32


def inverse(value):
    return pl.reciprocal(value, approx=False)


def root(value):
    return value * lax.rsqrt(value)


def faces(before, here, after, beyond):
    value = 7.0 / 12.0 * (here + after) - 1.0 / 12.0 * (before + beyond)
    return jnp.minimum(jnp.maximum(value, jnp.minimum(here, after)), jnp.maximum(here, after))


def parabola(here, lower, upper):
    rise, fall = here - lower, upper - here
    return rise + fall, rise - fall


def reaches(half_reach):
    return half_reach, 3.0 * half_reach - 4.0 * half_reach * half_reach


def riemann(mass_l, speed_l, press_l, mass_r, speed_r, press_r):
    mass_l, mass_r = jnp.maximum(mass_l, PRESSURE_FLOOR), jnp.maximum(mass_r, PRESSURE_FLOOR)
    press_l, press_r = jnp.maximum(press_l, PRESSURE_FLOOR), jnp.maximum(press_r, PRESSURE_FLOOR)
    gain_l = (ADIABATIC + 1.0) / ADIABATIC * inverse(press_l)
    gain_r = (ADIABATIC + 1.0) / ADIABATIC * inverse(press_r)
    light_l = lax.rsqrt(0.5 * ADIABATIC * press_l * mass_l)
    light_r = lax.rsqrt(0.5 * ADIABATIC * press_r * mass_r)
    rest = (ADIABATIC - 1.0) / ADIABATIC
    closing = speed_l - speed_r
    star = (press_l * light_l + press_r * light_r + 2.0**0.5 * closing) * inverse(light_l + light_r)
    star = jnp.maximum(star, PRESSURE_FLOOR)
    for _ in range(RITER):
        root_l = lax.rsqrt(gain_l * star + rest)
        root_r = lax.rsqrt(gain_r * star + rest)
        slow_l = root_l * light_l
        slow_r = root_r * light_r
        gap = closing - (star - press_l) * slow_l - (star - press_r) * slow_r
        bottom = slow_l * (root_l * root_l + 0.5) + slow_r * (root_r * root_r + 0.5)
        star = jnp.maximum(star + gap * inverse(bottom), PRESSURE_FLOOR)
    slow_l = lax.rsqrt(gain_l * star + rest) * light_l
    slow_r = lax.rsqrt(gain_r * star + rest) * light_r
    speed = speed_l * slow_r + speed_r * slow_l + (press_l - press_r) * (slow_l * slow_r)
    return star, speed * inverse(slow_l + slow_r)


def primitives(mass, moments, energy, normal, step):
    thin = inverse(mass)
    square = moments[0] * moments[0] + moments[1] * moments[1] + moments[2] * moments[2]
    press = jnp.maximum((ADIABATIC - 1.0) * (energy - 0.5 * square * thin), PRESSURE_FLOOR)
    return moments[normal] * thin, press, 0.5 * step * root(ADIABATIC * press * thin)


def interfaces(mass, speed, press, half_reach):
    n = mass.shape[0] - 5
    half, bent = reaches(half_reach[2 : n + 3])
    sides = []
    for value in (mass, speed, press):
        face = faces(value[: n + 2], value[1 : n + 3], value[2 : n + 4], value[3 : n + 5])
        lower, upper = face[: n + 1], face[1:]
        slope, curve = parabola(value[2 : n + 3], lower, upper)
        slope, curve = half * slope, bent * curve
        sides.append(((upper - slope + curve)[:n], (lower + slope + curve)[1:]))
    (mass_l, mass_r), (speed_l, speed_r), (press_l, press_r) = sides
    return riemann(mass_l, speed_l, press_l, mass_r, speed_r, press_r)


def remap(fields, normal, star, speed, step):
    n = star.shape[0] - 3
    shift = step * speed
    work = shift * star
    push = step * star
    thin = inverse(1.0 + (shift[1:] - shift[:-1]))
    amounts = list(fields)
    amounts[normal] = fields[normal] - (push[1:] - push[:-1])
    amounts[4] = fields[4] - (work[1:] - work[:-1])
    ahead = jnp.maximum(shift[1:-1], 0.0) * thin[:-1]
    back = jnp.minimum(shift[1:-1], 0.0) * thin[1:]
    keep = 1.0 - ahead[1:] + back[:-1]
    return [a[1 : n + 1] * keep + a[:n] * ahead[:-1] - a[2:] * back[1:] for a in amounts]


def shift_up(value):
    lane = lax.broadcasted_iota(jnp.int32, value.shape, 2)
    turned = pltpu.roll(value, LANES - 1, 2)
    groups = turned.reshape(-1, LINES, LINES, LANES)
    after = jnp.concatenate([groups[:, 1:], groups[:, :1]], axis=1).reshape(value.shape)
    return jnp.where(lane == LANES - 1, after, turned)


def shift_down(value):
    lane = lax.broadcasted_iota(jnp.int32, value.shape, 2)
    turned = pltpu.roll(value, 1, 2)
    groups = turned.reshape(-1, LINES, LINES, LANES)
    before = jnp.concatenate([groups[:, LINES - 1 :], groups[:, : LINES - 1]], axis=1).reshape(value.shape)
    return jnp.where(lane == 0, before, turned)


def prepare(mass, speeds, press):
    press = jnp.maximum(press, PRESSURE_FLOOR)
    square = speeds[0] * speeds[0] + speeds[1] * speeds[1] + speeds[2] * speeds[2]
    energy = 1.0 / (ADIABATIC - 1.0) * press + 0.5 * mass * square
    sound = root(ADIABATIC * press * inverse(mass))
    held = [mass, mass * speeds[0], mass * speeds[1], mass * speeds[2], energy, sound]
    for value in (mass, speeds[0], press):
        after = shift_up(value)
        face = faces(shift_down(value), value, after, shift_up(after))
        held.extend((face,) + parabola(value, shift_down(face), face))
    return held


def solve_x(sound, shapes, step):
    half, bent = reaches(0.5 * step * sound)
    sides = []
    for face, slope, curve in shapes:
        lower = face - slope
        slope, curve = half * slope, bent * curve
        sides.append((face - slope + curve, shift_up(lower + slope + curve)))
    (mass_l, mass_r), (speed_l, speed_r), (press_l, press_r) = sides
    return riemann(mass_l, speed_l, press_l, mass_r, speed_r, press_r)


def remap_x(fields, star, speed, step):
    shift = step * speed
    shift_low, star_low = shift_down(shift), shift_down(star)
    thin = inverse(1.0 + (shift - shift_low))
    amounts = list(fields)
    amounts[1] = fields[1] - step * (star - star_low)
    amounts[4] = fields[4] - (shift * star - shift_low * star_low)
    ahead = jnp.maximum(shift, 0.0) * thin
    back = jnp.minimum(shift, 0.0) * shift_up(thin)
    flux = [ahead * a + back * shift_up(a) for a in amounts]
    return [a - f + shift_down(f) for a, f in zip(amounts, flux)]


def survey_kernel(odd, density, velocity, pressure, speed, paired, other):
    mass, press = density[...], pressure[...]
    sound = ADIABATIC * press / mass
    largest = jnp.maximum(jnp.abs(velocity[0]), jnp.abs(velocity[1]))
    largest = jnp.maximum(largest, jnp.abs(velocity[2])) + root(sound)
    speed[...] = jnp.full(speed.shape, jnp.max(largest), F32)
    refs = (density, velocity.at[0], velocity.at[1], velocity.at[2], pressure)
    for index, ref in enumerate(refs):
        for tile in range(LINES):
            low = ref[pl.ds(tile * LINES, HALO), :]
            high = ref[pl.ds((ROWS - LINES + tile) * LINES + HALO, HALO), :]
            paired[index, tile] = jnp.where(odd[0, 0] == 1, low, high)
            other[index, tile] = jnp.where(odd[0, 0] == 1, high, low)


def step_of(speeds):
    return COURANT_NUMBER / jnp.broadcast_to(jnp.max(speeds[...], axis=0, keepdims=True), (LINES, LANES))


def blocks(total, size):
    return [slice(first, min(first + size, total)) for first in range(0, total, size)]


HELD = 15
Y_FACES = 35
Y_CELLS = 32


def to_lines(ref, tiles, rows):
    for place in range(tiles.shape[0]):
        group, line = rows.start // LINES + place // LINES, place % LINES
        if group < ROWS // LINES:
            ref[pl.ds((group * LINES + HALO) * LINES + line, LINES, stride=LINES), :] = tiles[place]
        else:
            ref[pl.ds(line, HALO, stride=LINES), :] = tiles[place, :HALO]
            ref[pl.ds((ROWS + HALO) * LINES + line, HALO, stride=LINES), :] = tiles[place, HALO:]


def sweep_x(held, step):
    star, speed = solve_x(held[5], (held[6:9], held[9:12], held[12:15]), step)
    new = remap_x(held[:5], star, speed, step)
    return new + list(primitives(new[0], new[1:4], new[4], 1, step))


def seat(column):
    return column ^ 4


def lines_of(ref, index, rows):
    return ref[index, rows.start * LINES : rows.stop * LINES].reshape(-1, LINES, LANES)


def sweep_y(lines, out, star, speed, step):
    for part in blocks(ROWS + 3, Y_FACES):
        rows = slice(part.start, part.stop + 5)
        star[part], speed[part] = interfaces(*(lines_of(lines, index, rows) for index in (0, 5, 6, 7)))
    for cells in blocks(ROWS, Y_CELLS):
        rows = slice(cells.start + HALO - 1, cells.stop + HALO + 1)
        near = slice(cells.start, cells.stop + 3)
        new = remap([lines_of(lines, index, rows) for index in range(5)], 2, star[near], speed[near], step)
        for index in range(5):
            pairs = new[index].reshape(-1, 2, LINES, LANES)
            for pair in range(pairs.shape[0]):
                out[seat(cells.start // 2 + pair), 2 * index : 2 * index + 2] = pairs[pair]


def raw_tiles(density, velocity, pressure):
    refs = (density, velocity.at[0], velocity.at[1], velocity.at[2], pressure)
    return [ref[...].reshape(-1, LINES, LANES) for ref in refs]


def prepare_kernel(density, velocity, pressure, held):
    inner = raw_tiles(density, velocity, pressure)
    for index, value in enumerate(prepare(inner[0], inner[1:4], inner[4])):
        held[index] = value


def plane_kernel(odd, top, held, paired, other, out, rim, lines, star, speed):
    step = step_of(top)
    for index in range(5):
        rim[index, :, :HALO] = jnp.where(odd[0, 0] == 1, paired[index], other[index])
        rim[index, :, HALO:] = jnp.where(odd[0, 0] == 1, other[index], paired[index])
    outer = prepare(rim[0], [rim[1], rim[2], rim[3]], rim[4])
    swept = sweep_x([jnp.concatenate([held[index], outer[index]], axis=0) for index in range(HELD)], step)
    for index in range(8):
        to_lines(lines.at[index], swept[index], slice(0, ROWS + 2 * HALO))
    sweep_y(lines, out, star, speed, step)


def column_kernel(top, lines, out):
    step = step_of(top)
    for row in range(2):
        fields = [jnp.stack([lines[seat(z), 2 * index + row] for z in range(DEPTH)]) for index in range(5)]
        along, press, half_reach = primitives(fields[0], fields[1:4], fields[4], 2, step)

        def ring(value, before, after):
            return jnp.concatenate([value[DEPTH - before :], value, value[:after]], axis=0)

        star_now, speed_now = interfaces(*(ring(value, 2, 3) for value in (fields[0], along, press, half_reach)))
        new = remap([ring(f, 1, 1) for f in fields], 3, ring(star_now, 2, 1), ring(speed_now, 2, 1), step)
        for index in range(5):
            for z in range(DEPTH):
                out[index, z, pl.ds(row, LINES, stride=2), :] = new[index][z]


def tiled(array):
    lead = array.shape[:-2]
    split = array.reshape(lead + (ROWS // LINES, LINES, LINES, LANES))
    return jnp.swapaxes(split, -3, -2).reshape(lead + (ROWS * LINES, LANES))


def swap_speeds(speeds, axes):
    order = list(range(speeds.shape[0]))[::-1]
    swapped = lax.all_to_all(speeds, axes, split_axis=0, concat_axis=0, tiled=True, axis_index_groups=[order])
    return swapped.reshape(-1, LANES)


def local(density, velocity, pressure, sizes):
    vmem = pl.BlockSpec(memory_space=pltpu.VMEM)
    smem = pl.BlockSpec(memory_space=pltpu.SMEM)
    wide = pltpu.CompilerParams(vmem_limit_bytes=32 * 1024 * 1024)
    density = tiled(density[0])
    velocity = tiled(velocity[:, 0])
    pressure = tiled(pressure[0])
    near = sizes["x"] * sizes["core"]
    far = sizes["y_hi"] * sizes["z"] * sizes["y_lo"]
    rows = sizes["y_hi"] * sizes["z"]
    halo = jax.ShapeDtypeStruct((5, LINES, HALO, LANES), F32)
    odd = (lax.axis_index("z") & 1).reshape(1, 1)
    fastest, paired, other = pl.pallas_call(
        survey_kernel,
        out_shape=(jax.ShapeDtypeStruct((far * 2, LANES), F32), halo, halo),
        in_specs=[smem] + [vmem] * 3,
        out_specs=(vmem, vmem, vmem),
        name="survey",
    )(odd, density, velocity, pressure)
    other = lax.ppermute(other, ROW, [(i, (i + i % 2 * 2 - 1) % rows) for i in range(rows)])
    paired = lax.ppermute(paired, ROW, [(i, i ^ 1) for i in range(rows)])
    fastest = swap_speeds(fastest.reshape(far, 2, LANES), ("y_hi", "z", "y_lo"))
    fastest = jnp.broadcast_to(jnp.max(fastest, axis=0, keepdims=True), (near, 1, LANES))
    fastest, density, velocity, pressure = lax.optimization_barrier((fastest, density, velocity, pressure))
    top = swap_speeds(fastest, ("x", "core"))
    held = pl.pallas_call(
        prepare_kernel,
        out_shape=jax.ShapeDtypeStruct((HELD, ROWS, LINES, LANES), F32),
        in_specs=[vmem] * 3,
        out_specs=vmem,
        compiler_params=pltpu.CompilerParams(vmem_limit_bytes=32 * 1024 * 1024),
        cost_estimate=pl.CostEstimate(flops=4000000, bytes_accessed=2600000, transcendentals=100000),
        name="prepare_rows",
    )(density, velocity, pressure)
    faces_shape = pltpu.VMEM((ROWS + 3, LINES, LANES), F32)
    rim_shape = pltpu.VMEM((5, LINES, LINES, LANES), F32)
    lines_shape = (8, (ROWS + 2 * HALO) * LINES, LANES)
    sent_shape = jax.ShapeDtypeStruct((DEPTH, 10, LINES, LANES), F32)
    lines = pl.pallas_call(
        plane_kernel,
        out_shape=sent_shape,
        in_specs=[smem] + [vmem] * 4,
        out_specs=vmem,
        scratch_shapes=[rim_shape, pltpu.VMEM(lines_shape, F32), faces_shape, faces_shape],
        compiler_params=wide,
        name="plane_sweeps",
    )(odd, top, held, paired, other)
    seats = [seat(column) for column in range(DEPTH)]
    lines = lax.all_to_all(lines, COL, split_axis=0, concat_axis=0, tiled=True, axis_index_groups=[seats])
    result = pl.pallas_call(
        column_kernel,
        out_shape=jax.ShapeDtypeStruct((5, DEPTH, 2 * LINES, LANES), F32),
        in_specs=[vmem, vmem],
        out_specs=vmem,
        compiler_params=wide,
        name="column_sweep",
    )(top, lines)
    return jnp.swapaxes(result.reshape(5, DEPTH, LINES, 2, LANES), 2, 3).reshape(5, DEPTH, 2, LINES * LANES)


ROW = ("y_hi", "z")
COL = ("y_lo", "x", "core")


def solution(mesh):
    rows, cols = mesh.shape["row"], mesh.shape["col"]
    sizes = {"y_hi": 4, "z": rows // 4, "y_lo": 2, "x": cols // 4, "core": 2}
    parts = jax.sharding.Mesh(mesh.devices.reshape(tuple(sizes.values())), ROW + COL)
    placed = (P(COL, ROW, None), P(None, COL, ROW, None), P(COL, ROW, None))

    def step(density, velocity, pressure):
        return local(density, velocity, pressure, sizes)

    return jax.shard_map(
        step,
        mesh=parts,
        in_specs=placed,
        out_specs=P(None, None, ROW + COL, None),
        check_vma=False,
    )
```

```python
import jax
import jax.numpy as jnp
from jax import lax
from jax.experimental import pallas as pl
from jax.experimental.pallas import tpu as pltpu
from jax.sharding import PartitionSpec as P

RITER = 5
ADIABATIC = 5.0 / 3.0
COURANT_NUMBER = 0.3
PRESSURE_FLOOR = 0.05

LINES = 8
LANES = 128
HALO = 4
ROWS = 32
DEPTH = 16
F32 = jnp.float32


def inverse(value):
    return pl.reciprocal(value, approx=False)


def root(value):
    return value * lax.rsqrt(value)


def faces(before, here, after, beyond):
    value = 7.0 / 12.0 * (here + after) - 1.0 / 12.0 * (before + beyond)
    return jnp.minimum(jnp.maximum(value, jnp.minimum(here, after)), jnp.maximum(here, after))


def parabola(here, lower, upper):
    rise, fall = here - lower, upper - here
    return rise + fall, rise - fall


def reaches(half_reach):
    return half_reach, 3.0 * half_reach - 4.0 * half_reach * half_reach


def riemann(mass_l, speed_l, press_l, mass_r, speed_r, press_r):
    mass_l, mass_r = jnp.maximum(mass_l, PRESSURE_FLOOR), jnp.maximum(mass_r, PRESSURE_FLOOR)
    press_l, press_r = jnp.maximum(press_l, PRESSURE_FLOOR), jnp.maximum(press_r, PRESSURE_FLOOR)
    gain_l = (ADIABATIC + 1.0) / ADIABATIC * inverse(press_l)
    gain_r = (ADIABATIC + 1.0) / ADIABATIC * inverse(press_r)
    light_l = lax.rsqrt(0.5 * ADIABATIC * press_l * mass_l)
    light_r = lax.rsqrt(0.5 * ADIABATIC * press_r * mass_r)
    rest = (ADIABATIC - 1.0) / ADIABATIC
    closing = speed_l - speed_r
    star = (press_l * light_l + press_r * light_r + 2.0**0.5 * closing) * inverse(light_l + light_r)
    star = jnp.maximum(star, PRESSURE_FLOOR)
    for _ in range(RITER):
        root_l = lax.rsqrt(gain_l * star + rest)
        root_r = lax.rsqrt(gain_r * star + rest)
        slow_l = root_l * light_l
        slow_r = root_r * light_r
        gap = closing - (star - press_l) * slow_l - (star - press_r) * slow_r
        bottom = slow_l * (root_l * root_l + 0.5) + slow_r * (root_r * root_r + 0.5)
        star = jnp.maximum(star + gap * inverse(bottom), PRESSURE_FLOOR)
    slow_l = lax.rsqrt(gain_l * star + rest) * light_l
    slow_r = lax.rsqrt(gain_r * star + rest) * light_r
    speed = speed_l * slow_r + speed_r * slow_l + (press_l - press_r) * (slow_l * slow_r)
    return star, speed * inverse(slow_l + slow_r)


def primitives(mass, moments, energy, normal, step):
    thin = inverse(mass)
    square = moments[0] * moments[0] + moments[1] * moments[1] + moments[2] * moments[2]
    press = jnp.maximum((ADIABATIC - 1.0) * (energy - 0.5 * square * thin), PRESSURE_FLOOR)
    return moments[normal] * thin, press, 0.5 * step * root(ADIABATIC * press * thin)


def interfaces(mass, speed, press, half_reach):
    n = mass.shape[0] - 5
    half, bent = reaches(half_reach[2 : n + 3])
    sides = []
    for value in (mass, speed, press):
        face = faces(value[: n + 2], value[1 : n + 3], value[2 : n + 4], value[3 : n + 5])
        lower, upper = face[: n + 1], face[1:]
        slope, curve = parabola(value[2 : n + 3], lower, upper)
        slope, curve = half * slope, bent * curve
        sides.append(((upper - slope + curve)[:n], (lower + slope + curve)[1:]))
    (mass_l, mass_r), (speed_l, speed_r), (press_l, press_r) = sides
    return riemann(mass_l, speed_l, press_l, mass_r, speed_r, press_r)


def remap(fields, normal, star, speed, step):
    n = star.shape[0] - 3
    shift = step * speed
    work = shift * star
    push = step * star
    thin = inverse(1.0 + (shift[1:] - shift[:-1]))
    amounts = list(fields)
    amounts[normal] = fields[normal] - (push[1:] - push[:-1])
    amounts[4] = fields[4] - (work[1:] - work[:-1])
    ahead = jnp.maximum(shift[1:-1], 0.0) * thin[:-1]
    back = jnp.minimum(shift[1:-1], 0.0) * thin[1:]
    keep = 1.0 - ahead[1:] + back[:-1]
    return [a[1 : n + 1] * keep + a[:n] * ahead[:-1] - a[2:] * back[1:] for a in amounts]


def shift_up(value):
    lane = lax.broadcasted_iota(jnp.int32, value.shape, 2)
    turned = pltpu.roll(value, LANES - 1, 2)
    groups = turned.reshape(-1, LINES, LINES, LANES)
    after = jnp.concatenate([groups[:, 1:], groups[:, :1]], axis=1).reshape(value.shape)
    return jnp.where(lane == LANES - 1, after, turned)


def shift_down(value):
    lane = lax.broadcasted_iota(jnp.int32, value.shape, 2)
    turned = pltpu.roll(value, 1, 2)
    groups = turned.reshape(-1, LINES, LINES, LANES)
    before = jnp.concatenate([groups[:, LINES - 1 :], groups[:, : LINES - 1]], axis=1).reshape(value.shape)
    return jnp.where(lane == 0, before, turned)


def prepare(mass, speeds, press):
    press = jnp.maximum(press, PRESSURE_FLOOR)
    square = speeds[0] * speeds[0] + speeds[1] * speeds[1] + speeds[2] * speeds[2]
    energy = 1.0 / (ADIABATIC - 1.0) * press + 0.5 * mass * square
    sound = root(ADIABATIC * press * inverse(mass))
    held = [mass, mass * speeds[0], mass * speeds[1], mass * speeds[2], energy, sound]
    for value in (mass, speeds[0], press):
        after = shift_up(value)
        face = faces(shift_down(value), value, after, shift_up(after))
        held.extend((face,) + parabola(value, shift_down(face), face))
    return held


def solve_x(sound, shapes, step):
    half, bent = reaches(0.5 * step * sound)
    sides = []
    for face, slope, curve in shapes:
        lower = face - slope
        slope, curve = half * slope, bent * curve
        sides.append((face - slope + curve, shift_up(lower + slope + curve)))
    (mass_l, mass_r), (speed_l, speed_r), (press_l, press_r) = sides
    return riemann(mass_l, speed_l, press_l, mass_r, speed_r, press_r)


def remap_x(fields, star, speed, step):
    shift = step * speed
    shift_low, star_low = shift_down(shift), shift_down(star)
    thin = inverse(1.0 + (shift - shift_low))
    amounts = list(fields)
    amounts[1] = fields[1] - step * (star - star_low)
    amounts[4] = fields[4] - (shift * star - shift_low * star_low)
    ahead = jnp.maximum(shift, 0.0) * thin
    back = jnp.minimum(shift, 0.0) * shift_up(thin)
    flux = [ahead * a + back * shift_up(a) for a in amounts]
    return [a - f + shift_down(f) for a, f in zip(amounts, flux)]


def survey_kernel(odd, density, velocity, pressure, speed, paired, other, kept):
    mass, press = density[...], pressure[...]
    sound = ADIABATIC * press / mass
    largest = jnp.maximum(jnp.abs(velocity[0]), jnp.abs(velocity[1]))
    largest = jnp.maximum(largest, jnp.abs(velocity[2])) + root(sound)
    speed[...] = jnp.full(speed.shape, jnp.max(largest), F32)
    for index, value in enumerate(raw_tiles(density, velocity, pressure)):
        kept[index] = value
    refs = (density, velocity.at[0], velocity.at[1], velocity.at[2], pressure)
    for index, ref in enumerate(refs):
        for tile in range(LINES):
            low = ref[pl.ds(tile * LINES, HALO), :]
            high = ref[pl.ds((ROWS - LINES + tile) * LINES + HALO, HALO), :]
            paired[index, tile] = jnp.where(odd[0, 0] == 1, low, high)
            other[index, tile] = jnp.where(odd[0, 0] == 1, high, low)


def step_of(speeds):
    return COURANT_NUMBER / jnp.broadcast_to(jnp.max(speeds[...], axis=0, keepdims=True), (LINES, LANES))


def blocks(total, size):
    return [slice(first, min(first + size, total)) for first in range(0, total, size)]


HELD = 15
Y_FACES = 35
Y_CELLS = 32


def to_lines(ref, tiles, rows):
    for place in range(tiles.shape[0]):
        group, line = rows.start // LINES + place // LINES, place % LINES
        if group < ROWS // LINES:
            ref[pl.ds((group * LINES + HALO) * LINES + line, LINES, stride=LINES), :] = tiles[place]
        else:
            ref[pl.ds(line, HALO, stride=LINES), :] = tiles[place, :HALO]
            ref[pl.ds((ROWS + HALO) * LINES + line, HALO, stride=LINES), :] = tiles[place, HALO:]


def sweep_x(held, step):
    star, speed = solve_x(held[5], (held[6:9], held[9:12], held[12:15]), step)
    new = remap_x(held[:5], star, speed, step)
    return new + list(primitives(new[0], new[1:4], new[4], 1, step))


def seat(column):
    return column ^ 13


def lines_of(ref, index, rows):
    return ref[index, rows.start * LINES : rows.stop * LINES].reshape(-1, LINES, LANES)


def sweep_y(lines, out, star, speed, step):
    for part in blocks(ROWS + 3, Y_FACES):
        rows = slice(part.start, part.stop + 5)
        star[part], speed[part] = interfaces(*(lines_of(lines, index, rows) for index in (0, 5, 6, 7)))
    for cells in blocks(ROWS, Y_CELLS):
        rows = slice(cells.start + HALO - 1, cells.stop + HALO + 1)
        near = slice(cells.start, cells.stop + 3)
        new = remap([lines_of(lines, index, rows) for index in range(5)], 2, star[near], speed[near], step)
        for index in range(5):
            pairs = new[index].reshape(-1, 2, LINES, LANES)
            for pair in range(pairs.shape[0]):
                out[seat(cells.start // 2 + pair), 2 * index : 2 * index + 2] = pairs[pair]


def raw_tiles(density, velocity, pressure):
    refs = (density, velocity.at[0], velocity.at[1], velocity.at[2], pressure)
    return [ref[...].reshape(-1, LINES, LANES) for ref in refs]


def prepare_kernel(arrived, kept, held):
    for index, value in enumerate(prepare(kept[0], [kept[1], kept[2], kept[3]], kept[4])):
        held[index] = value


def plane_kernel(odd, top, held, paired, other, out, rim, lines, star, speed):
    step = step_of(top)
    for index in range(5):
        rim[index, :, :HALO] = jnp.where(odd[0, 0] == 1, paired[index], other[index])
        rim[index, :, HALO:] = jnp.where(odd[0, 0] == 1, other[index], paired[index])
    outer = prepare(rim[0], [rim[1], rim[2], rim[3]], rim[4])
    swept = sweep_x([jnp.concatenate([held[index], outer[index]], axis=0) for index in range(HELD)], step)
    for index in range(8):
        to_lines(lines.at[index], swept[index], slice(0, ROWS + 2 * HALO))
    sweep_y(lines, out, star, speed, step)


def column_kernel(top, lines, out):
    step = step_of(top)
    for row in range(2):
        fields = [jnp.stack([lines[seat(z), 2 * index + row] for z in range(DEPTH)]) for index in range(5)]
        along, press, half_reach = primitives(fields[0], fields[1:4], fields[4], 2, step)

        def ring(value, before, after):
            return jnp.concatenate([value[DEPTH - before :], value, value[:after]], axis=0)

        star_now, speed_now = interfaces(*(ring(value, 2, 3) for value in (fields[0], along, press, half_reach)))
        new = remap([ring(f, 1, 1) for f in fields], 3, ring(star_now, 2, 1), ring(speed_now, 2, 1), step)
        for index in range(5):
            for z in range(DEPTH):
                out[index, z, pl.ds(row, LINES, stride=2), :] = new[index][z]


def tiled(array):
    lead = array.shape[:-2]
    split = array.reshape(lead + (ROWS // LINES, LINES, LINES, LANES))
    return jnp.swapaxes(split, -3, -2).reshape(lead + (ROWS * LINES, LANES))


def swap_speeds(speeds, axes):
    order = list(range(speeds.shape[0]))[::-1]
    swapped = lax.all_to_all(speeds, axes, split_axis=0, concat_axis=0, tiled=True, axis_index_groups=[order])
    return swapped.reshape(-1, LANES)


def local(density, velocity, pressure, sizes):
    vmem = pl.BlockSpec(memory_space=pltpu.VMEM)
    smem = pl.BlockSpec(memory_space=pltpu.SMEM)
    wide = pltpu.CompilerParams(vmem_limit_bytes=32 * 1024 * 1024)
    density = tiled(density[0])
    velocity = tiled(velocity[:, 0])
    pressure = tiled(pressure[0])
    near = sizes["x"] * sizes["core"]
    far = sizes["y_hi"] * sizes["z"] * sizes["y_lo"]
    rows = sizes["y_hi"] * sizes["z"]
    kept_shape = pltpu.VMEM((5, ROWS, LINES, LANES), F32)
    halo = jax.ShapeDtypeStruct((5, LINES, HALO, LANES), F32)
    odd = (lax.axis_index("z") & 1).reshape(1, 1)
    fastest, paired, other, kept = pl.pallas_call(
        survey_kernel,
        out_shape=(jax.ShapeDtypeStruct((far * 2, LANES), F32), halo, halo, kept_shape),
        in_specs=[smem] + [vmem] * 3,
        out_specs=(vmem, vmem, vmem, vmem),
        name="survey",
    )(odd, density, velocity, pressure)
    other = lax.ppermute(other, ROW, [(i, (i + i % 2 * 2 - 1) % rows) for i in range(rows)])
    paired = lax.ppermute(paired, ROW, [(i, i ^ 1) for i in range(rows)])
    fastest = swap_speeds(fastest.reshape(far, 2, LANES), ("y_hi", "z", "y_lo"))
    fastest = jnp.broadcast_to(jnp.max(fastest, axis=0, keepdims=True), (near, 1, LANES))
    held = pl.pallas_call(
        prepare_kernel,
        out_shape=jax.ShapeDtypeStruct((HELD, ROWS, LINES, LANES), F32),
        in_specs=[pl.BlockSpec(memory_space=pl.ANY), vmem],
        out_specs=vmem,
        compiler_params=wide,
        cost_estimate=pl.CostEstimate(flops=4000000, bytes_accessed=2600000, transcendentals=100000),
        name="prepare_rows",
    )(paired, kept)
    fastest, held = lax.optimization_barrier((fastest, held))
    top = swap_speeds(fastest, ("x", "core"))
    faces_shape = pltpu.VMEM((ROWS + 3, LINES, LANES), F32)
    rim_shape = pltpu.VMEM((5, LINES, LINES, LANES), F32)
    lines_shape = (8, (ROWS + 2 * HALO) * LINES, LANES)
    sent_shape = jax.ShapeDtypeStruct((DEPTH, 10, LINES, LANES), F32)
    lines = pl.pallas_call(
        plane_kernel,
        out_shape=sent_shape,
        in_specs=[smem] + [vmem] * 4,
        out_specs=vmem,
        scratch_shapes=[rim_shape, pltpu.VMEM(lines_shape, F32), faces_shape, faces_shape],
        compiler_params=wide,
        name="plane_sweeps",
    )(odd, top, held, paired, other)
    seats = [seat(column) for column in range(DEPTH)]
    lines = lax.all_to_all(lines, COL, split_axis=0, concat_axis=0, tiled=True, axis_index_groups=[seats])
    result = pl.pallas_call(
        column_kernel,
        out_shape=jax.ShapeDtypeStruct((5, DEPTH, 2 * LINES, LANES), F32),
        in_specs=[vmem, vmem],
        out_specs=vmem,
        compiler_params=wide,
        name="column_sweep",
    )(top, lines)
    return jnp.swapaxes(result.reshape(5, DEPTH, LINES, 2, LANES), 2, 3).reshape(5, DEPTH, 2, LINES * LANES)


ROW = ("y_hi", "z")
COL = ("y_lo", "x", "core")


def solution(mesh):
    rows, cols = mesh.shape["row"], mesh.shape["col"]
    sizes = {"y_hi": 4, "z": rows // 4, "y_lo": 2, "x": cols // 4, "core": 2}
    parts = jax.sharding.Mesh(mesh.devices.reshape(tuple(sizes.values())), ROW + COL)
    placed = (P(COL, ROW, None), P(None, COL, ROW, None), P(COL, ROW, None))

    def step(density, velocity, pressure):
        return local(density, velocity, pressure, sizes)

    return jax.shard_map(
        step,
        mesh=parts,
        in_specs=placed,
        out_specs=P(None, None, ROW + COL, None),
        check_vma=False,
    )
```

```python
import jax
import jax.numpy as jnp
from jax import lax
from jax.experimental import pallas as pl
from jax.experimental.pallas import tpu as pltpu
from jax.sharding import PartitionSpec as P

RITER = 5
ADIABATIC = 5.0 / 3.0
COURANT_NUMBER = 0.3
PRESSURE_FLOOR = 0.05

LINES = 8
LANES = 128
HALO = 4
ROWS = 32
DEPTH = 16
F32 = jnp.float32


def inverse(value):
    return pl.reciprocal(value, approx=False)


def root(value):
    return value * lax.rsqrt(value)


def faces(before, here, after, beyond):
    value = 7.0 / 12.0 * (here + after) - 1.0 / 12.0 * (before + beyond)
    return jnp.minimum(jnp.maximum(value, jnp.minimum(here, after)), jnp.maximum(here, after))


def parabola(here, lower, upper):
    rise, fall = here - lower, upper - here
    return rise + fall, rise - fall


def reaches(half_reach):
    return half_reach, 3.0 * half_reach - 4.0 * half_reach * half_reach


def riemann(mass_l, speed_l, press_l, mass_r, speed_r, press_r):
    mass_l, mass_r = jnp.maximum(mass_l, PRESSURE_FLOOR), jnp.maximum(mass_r, PRESSURE_FLOOR)
    press_l, press_r = jnp.maximum(press_l, PRESSURE_FLOOR), jnp.maximum(press_r, PRESSURE_FLOOR)
    gain_l = (ADIABATIC + 1.0) / ADIABATIC * inverse(press_l)
    gain_r = (ADIABATIC + 1.0) / ADIABATIC * inverse(press_r)
    light_l = lax.rsqrt(0.5 * ADIABATIC * press_l * mass_l)
    light_r = lax.rsqrt(0.5 * ADIABATIC * press_r * mass_r)
    rest = (ADIABATIC - 1.0) / ADIABATIC
    closing = speed_l - speed_r
    star = (press_l * light_l + press_r * light_r + 2.0**0.5 * closing) * inverse(light_l + light_r)
    star = jnp.maximum(star, PRESSURE_FLOOR)
    for _ in range(RITER):
        root_l = lax.rsqrt(gain_l * star + rest)
        root_r = lax.rsqrt(gain_r * star + rest)
        slow_l = root_l * light_l
        slow_r = root_r * light_r
        gap = closing - (star - press_l) * slow_l - (star - press_r) * slow_r
        bottom = slow_l * (root_l * root_l + 0.5) + slow_r * (root_r * root_r + 0.5)
        star = jnp.maximum(star + gap * inverse(bottom), PRESSURE_FLOOR)
    slow_l = lax.rsqrt(gain_l * star + rest) * light_l
    slow_r = lax.rsqrt(gain_r * star + rest) * light_r
    speed = speed_l * slow_r + speed_r * slow_l + (press_l - press_r) * (slow_l * slow_r)
    return star, speed * inverse(slow_l + slow_r)


def primitives(mass, moments, energy, normal, step):
    thin = inverse(mass)
    square = moments[0] * moments[0] + moments[1] * moments[1] + moments[2] * moments[2]
    press = jnp.maximum((ADIABATIC - 1.0) * (energy - 0.5 * square * thin), PRESSURE_FLOOR)
    return moments[normal] * thin, press, 0.5 * step * root(ADIABATIC * press * thin)


def interfaces(mass, speed, press, half_reach):
    n = mass.shape[0] - 5
    half, bent = reaches(half_reach[2 : n + 3])
    sides = []
    for value in (mass, speed, press):
        face = faces(value[: n + 2], value[1 : n + 3], value[2 : n + 4], value[3 : n + 5])
        lower, upper = face[: n + 1], face[1:]
        slope, curve = parabola(value[2 : n + 3], lower, upper)
        slope, curve = half * slope, bent * curve
        sides.append(((upper - slope + curve)[:n], (lower + slope + curve)[1:]))
    (mass_l, mass_r), (speed_l, speed_r), (press_l, press_r) = sides
    return riemann(mass_l, speed_l, press_l, mass_r, speed_r, press_r)


def remap(fields, normal, star, speed, step):
    n = star.shape[0] - 3
    shift = step * speed
    work = shift * star
    push = step * star
    thin = inverse(1.0 + (shift[1:] - shift[:-1]))
    amounts = list(fields)
    amounts[normal] = fields[normal] - (push[1:] - push[:-1])
    amounts[4] = fields[4] - (work[1:] - work[:-1])
    ahead = jnp.maximum(shift[1:-1], 0.0) * thin[:-1]
    back = jnp.minimum(shift[1:-1], 0.0) * thin[1:]
    keep = 1.0 - ahead[1:] + back[:-1]
    return [a[1 : n + 1] * keep + a[:n] * ahead[:-1] - a[2:] * back[1:] for a in amounts]


def shift_up(value):
    lane = lax.broadcasted_iota(jnp.int32, value.shape, 2)
    turned = pltpu.roll(value, LANES - 1, 2)
    groups = turned.reshape(-1, LINES, LINES, LANES)
    after = jnp.concatenate([groups[:, 1:], groups[:, :1]], axis=1).reshape(value.shape)
    return jnp.where(lane == LANES - 1, after, turned)


def shift_down(value):
    lane = lax.broadcasted_iota(jnp.int32, value.shape, 2)
    turned = pltpu.roll(value, 1, 2)
    groups = turned.reshape(-1, LINES, LINES, LANES)
    before = jnp.concatenate([groups[:, LINES - 1 :], groups[:, : LINES - 1]], axis=1).reshape(value.shape)
    return jnp.where(lane == 0, before, turned)


def prepare(mass, speeds, press):
    press = jnp.maximum(press, PRESSURE_FLOOR)
    square = speeds[0] * speeds[0] + speeds[1] * speeds[1] + speeds[2] * speeds[2]
    energy = 1.0 / (ADIABATIC - 1.0) * press + 0.5 * mass * square
    sound = root(ADIABATIC * press * inverse(mass))
    held = [mass, mass * speeds[0], mass * speeds[1], mass * speeds[2], energy, sound]
    for value in (mass, speeds[0], press):
        after = shift_up(value)
        face = faces(shift_down(value), value, after, shift_up(after))
        held.extend((face,) + parabola(value, shift_down(face), face))
    return held


def solve_x(sound, shapes, step):
    half, bent = reaches(0.5 * step * sound)
    sides = []
    for face, slope, curve in shapes:
        lower = face - slope
        slope, curve = half * slope, bent * curve
        sides.append((face - slope + curve, shift_up(lower + slope + curve)))
    (mass_l, mass_r), (speed_l, speed_r), (press_l, press_r) = sides
    return riemann(mass_l, speed_l, press_l, mass_r, speed_r, press_r)


def remap_x(fields, star, speed, step):
    shift = step * speed
    shift_low, star_low = shift_down(shift), shift_down(star)
    thin = inverse(1.0 + (shift - shift_low))
    amounts = list(fields)
    amounts[1] = fields[1] - step * (star - star_low)
    amounts[4] = fields[4] - (shift * star - shift_low * star_low)
    ahead = jnp.maximum(shift, 0.0) * thin
    back = jnp.minimum(shift, 0.0) * shift_up(thin)
    flux = [ahead * a + back * shift_up(a) for a in amounts]
    return [a - f + shift_down(f) for a, f in zip(amounts, flux)]


def survey_kernel(odd, density, velocity, pressure, speed, paired, other, kept):
    mass, press = density[...], pressure[...]
    sound = ADIABATIC * press / mass
    largest = jnp.maximum(jnp.abs(velocity[0]), jnp.abs(velocity[1]))
    largest = jnp.maximum(largest, jnp.abs(velocity[2])) + root(sound)
    speed[...] = jnp.full(speed.shape, jnp.max(largest), F32)
    for index, value in enumerate(raw_tiles(density, velocity, pressure)):
        kept[index] = value
    refs = (density, velocity.at[0], velocity.at[1], velocity.at[2], pressure)
    for index, ref in enumerate(refs):
        for tile in range(LINES):
            low = ref[pl.ds(tile * LINES, HALO), :]
            high = ref[pl.ds((ROWS - LINES + tile) * LINES + HALO, HALO), :]
            paired[index, tile] = jnp.where(odd[0, 0] == 1, low, high)
            other[index, tile] = jnp.where(odd[0, 0] == 1, high, low)


def step_of(speeds):
    return COURANT_NUMBER / jnp.broadcast_to(jnp.max(speeds[...], axis=0, keepdims=True), (LINES, LANES))


def blocks(total, size):
    return [slice(first, min(first + size, total)) for first in range(0, total, size)]


HELD = 15
Y_FACES = 35
Y_CELLS = 32


def to_lines(ref, tiles, rows):
    for place in range(tiles.shape[0]):
        group, line = rows.start // LINES + place // LINES, place % LINES
        if group < ROWS // LINES:
            ref[pl.ds((group * LINES + HALO) * LINES + line, LINES, stride=LINES), :] = tiles[place]
        else:
            ref[pl.ds(line, HALO, stride=LINES), :] = tiles[place, :HALO]
            ref[pl.ds((ROWS + HALO) * LINES + line, HALO, stride=LINES), :] = tiles[place, HALO:]


def sweep_x(held, step):
    star, speed = solve_x(held[5], (held[6:9], held[9:12], held[12:15]), step)
    new = remap_x(held[:5], star, speed, step)
    return new + list(primitives(new[0], new[1:4], new[4], 1, step))


def seat(column):
    return column ^ 13


def lines_of(ref, index, rows):
    return ref[index, rows.start * LINES : rows.stop * LINES].reshape(-1, LINES, LANES)


def sweep_y(lines, out, star, speed, step):
    for part in blocks(ROWS + 3, Y_FACES):
        rows = slice(part.start, part.stop + 5)
        star[part], speed[part] = interfaces(*(lines_of(lines, index, rows) for index in (0, 5, 6, 7)))
    for cells in blocks(ROWS, Y_CELLS):
        rows = slice(cells.start + HALO - 1, cells.stop + HALO + 1)
        near = slice(cells.start, cells.stop + 3)
        new = remap([lines_of(lines, index, rows) for index in range(5)], 2, star[near], speed[near], step)
        for index in range(5):
            pairs = new[index].reshape(-1, 2, LINES, LANES)
            for pair in range(pairs.shape[0]):
                out[seat(cells.start // 2 + pair), 2 * index : 2 * index + 2] = pairs[pair]


def raw_tiles(density, velocity, pressure):
    refs = (density, velocity.at[0], velocity.at[1], velocity.at[2], pressure)
    return [ref[...].reshape(-1, LINES, LANES) for ref in refs]


def prepare_kernel(arrived, kept, held):
    for index, value in enumerate(prepare(kept[0], [kept[1], kept[2], kept[3]], kept[4])):
        held[index] = value


def plane_kernel(odd, top, held, paired, other, out, rim, lines, star, speed):
    step = step_of(top)
    for index in range(5):
        rim[index, :, :HALO] = jnp.where(odd[0, 0] == 1, paired[index], other[index])
        rim[index, :, HALO:] = jnp.where(odd[0, 0] == 1, other[index], paired[index])
    outer = prepare(rim[0], [rim[1], rim[2], rim[3]], rim[4])
    swept = sweep_x([jnp.concatenate([held[index], outer[index]], axis=0) for index in range(HELD)], step)
    for index in range(8):
        to_lines(lines.at[index], swept[index], slice(0, ROWS + 2 * HALO))
    sweep_y(lines, out, star, speed, step)


def column_kernel(top, lines, out, done, sems):
    step = step_of(top)

    def ring(value, before, after):
        return jnp.concatenate([value[DEPTH - before :], value, value[:after]], axis=0)

    new = []
    for row in range(2):
        fields = [jnp.stack([lines[seat(z), 2 * index + row] for z in range(DEPTH)]) for index in range(5)]
        along, press, half_reach = primitives(fields[0], fields[1:4], fields[4], 2, step)
        star, speed = interfaces(*(ring(value, 2, 3) for value in (fields[0], along, press, half_reach)))
        new.append(remap([ring(f, 1, 1) for f in fields], 3, ring(star, 2, 1), ring(speed, 2, 1), step))
    copies = []
    for index in range(5):
        for row in range(2):
            for z in range(DEPTH):
                done[index, z, pl.ds(row, LINES, stride=2), :] = new[row][index][z]
        copies.append(pltpu.make_async_copy(done.at[index], out.at[index], sems.at[index]))
        copies[-1].start()
    for copy in copies:
        copy.wait()


def tiled(array):
    lead = array.shape[:-2]
    split = array.reshape(lead + (ROWS // LINES, LINES, LINES, LANES))
    return jnp.swapaxes(split, -3, -2).reshape(lead + (ROWS * LINES, LANES))


def swap_speeds(speeds, axes):
    order = list(range(speeds.shape[0]))[::-1]
    swapped = lax.all_to_all(speeds, axes, split_axis=0, concat_axis=0, tiled=True, axis_index_groups=[order])
    return swapped.reshape(-1, LANES)


def local(density, velocity, pressure, sizes):
    vmem = pl.BlockSpec(memory_space=pltpu.VMEM)
    smem = pl.BlockSpec(memory_space=pltpu.SMEM)
    wide = pltpu.CompilerParams(vmem_limit_bytes=32 * 1024 * 1024)
    density = tiled(density[0])
    velocity = tiled(velocity[:, 0])
    pressure = tiled(pressure[0])
    near = sizes["x"] * sizes["core"]
    far = sizes["y_hi"] * sizes["z"] * sizes["y_lo"]
    rows = sizes["y_hi"] * sizes["z"]
    kept_shape = pltpu.VMEM((5, ROWS, LINES, LANES), F32)
    halo = jax.ShapeDtypeStruct((5, LINES, HALO, LANES), F32)
    odd = (lax.axis_index("z") & 1).reshape(1, 1)
    fastest, paired, other, kept = pl.pallas_call(
        survey_kernel,
        out_shape=(jax.ShapeDtypeStruct((far * 2, LANES), F32), halo, halo, kept_shape),
        in_specs=[smem] + [vmem] * 3,
        out_specs=(vmem, vmem, vmem, vmem),
        name="survey",
    )(odd, density, velocity, pressure)
    other = lax.ppermute(other, ROW, [(i, (i + i % 2 * 2 - 1) % rows) for i in range(rows)])
    paired = lax.ppermute(paired, ROW, [(i, i ^ 1) for i in range(rows)])
    fastest = swap_speeds(fastest.reshape(far, 2, LANES), ("y_hi", "z", "y_lo"))
    fastest = jnp.broadcast_to(jnp.max(fastest, axis=0, keepdims=True), (near, 1, LANES))
    held = pl.pallas_call(
        prepare_kernel,
        out_shape=jax.ShapeDtypeStruct((HELD, ROWS, LINES, LANES), F32),
        in_specs=[pl.BlockSpec(memory_space=pl.ANY), vmem],
        out_specs=vmem,
        compiler_params=wide,
        cost_estimate=pl.CostEstimate(flops=4000000, bytes_accessed=2600000, transcendentals=100000),
        name="prepare_rows",
    )(paired, kept)
    fastest, held = lax.optimization_barrier((fastest, held))
    top = swap_speeds(fastest, ("x", "core"))
    faces_shape = pltpu.VMEM((ROWS + 3, LINES, LANES), F32)
    rim_shape = pltpu.VMEM((5, LINES, LINES, LANES), F32)
    lines_shape = (8, (ROWS + 2 * HALO) * LINES, LANES)
    sent_shape = jax.ShapeDtypeStruct((DEPTH, 10, LINES, LANES), F32)
    lines = pl.pallas_call(
        plane_kernel,
        out_shape=sent_shape,
        in_specs=[smem] + [vmem] * 4,
        out_specs=vmem,
        scratch_shapes=[rim_shape, pltpu.VMEM(lines_shape, F32), faces_shape, faces_shape],
        compiler_params=wide,
        name="plane_sweeps",
    )(odd, top, held, paired, other)
    seats = [seat(column) for column in range(DEPTH)]
    lines = lax.all_to_all(lines, COL, split_axis=0, concat_axis=0, tiled=True, axis_index_groups=[seats])
    result = pl.pallas_call(
        column_kernel,
        out_shape=jax.ShapeDtypeStruct((5, DEPTH, 2 * LINES, LANES), F32),
        in_specs=[vmem, vmem],
        out_specs=pl.BlockSpec(memory_space=pl.ANY),
        scratch_shapes=[
            pltpu.VMEM((5, DEPTH, 2 * LINES, LANES), F32),
            pltpu.SemaphoreType.DMA((5,)),
        ],
        compiler_params=wide,
        name="column_sweep",
    )(top, lines)
    return jnp.swapaxes(result.reshape(5, DEPTH, LINES, 2, LANES), 2, 3).reshape(5, DEPTH, 2, LINES * LANES)


ROW = ("y_hi", "z")
COL = ("y_lo", "x", "core")


def solution(mesh):
    rows, cols = mesh.shape["row"], mesh.shape["col"]
    sizes = {"y_hi": 4, "z": rows // 4, "y_lo": 2, "x": cols // 4, "core": 2}
    parts = jax.sharding.Mesh(mesh.devices.reshape(tuple(sizes.values())), ROW + COL)
    placed = (P(COL, ROW, None), P(None, COL, ROW, None), P(COL, ROW, None))

    def step(density, velocity, pressure):
        return local(density, velocity, pressure, sizes)

    return jax.shard_map(
        step,
        mesh=parts,
        in_specs=placed,
        out_specs=P(None, None, ROW + COL, None),
        check_vma=False,
    )
```
